32 devices in a mesh: grp: 2 (over y), wid: 4 (over z), hid: 4 (over x, core).
Axes of the slice: x: 2, y: 2, z: 4, core: 2. Of those that a mesh axis runs over, the one named last changes fastest.
Arguments:
- tokens: bfloat16 [1024, 6144], P(('grp', 'wid')), parts along dimension 0, may hold values from -6 to 6
- gate_weight: bfloat16 [2, 6144, 16384], P(None, None, ('hid', 'wid')), may hold values from -0.078125 to 0.078125
- up_weight: bfloat16 [2, 6144, 16384], P(None, None, ('hid', 'wid')), may hold values from -0.078125 to 0.078125
- down_weight: bfloat16 [2, 16384, 6144], P(None, 'hid', 'wid'), may hold values from -0.046875 to 0.046875
- routes: int32 [8, 2], P('grp'), parts along dimension 0, may hold values from 0 to 7, as said below
- combine: float32 [1024, 2], P('grp'), parts along dimension 0, may hold values from 0.2 to 1
Outputs:
- mixed: bfloat16 [1024, 6144], P(('grp', 'hid'), 'wid'), parts along dimension 0
The draws below stay inside these ranges and needn't reach their ends.
There are 2 independent parts, one for each index of `grp`. The reference program is written for one: setup_inputs(seed, part) draws one part's arguments, and reference() takes and returns one part's arrays. A program takes and returns all parts, laid end to end along the dimension named above; an argument that names none is the same for every part. Nothing has to cross between parts.
Inputs may be any that keep to these rules, and one draw needn't show every extreme that they name: `routes`: the two ids of a block differ. Ids below 2 are the held experts; at least one block names one of them.
All inputs are finite; a program needn't handle non-finite values.
Results may differ from the reference program's by a relative error of at most 0.005.
Values may be sent and summed in bfloat16 or wider, within the bound.
No kernel may reach another device: no remote copies, remote signals or barrier semaphores. Data moves between devices by JAX's collectives and lax.ppermute only.
A program may use at most 192 MiB of HBM per device.

```python
import jax
import jax.numpy as jnp

D = 6144
FF = 16384
ROUTED = 8
EXPERTS = 2
BLOCKS = 4
TOKENS = 512


def draw_routes(key, part):
    key = jax.random.fold_in(key, 7)
    keys = jax.random.split(key, 4)
    first = jax.random.randint(keys[0], (BLOCKS,), 0, ROUTED)
    offset = jax.random.randint(keys[1], (BLOCKS,), 1, ROUTED)
    second = (first + offset) % ROUTED
    chosen = jax.random.randint(keys[2], (), 0, BLOCKS)
    inside = jax.random.randint(keys[3], (), 0, EXPERTS)
    first = jnp.where(jnp.arange(BLOCKS) == chosen, inside, first)
    second = jnp.where(second == first, (second + 1) % ROUTED, second)
    return jnp.stack([first, second], axis=1).astype(jnp.int32)


def steps_of(key, extent, cuts, low, top_value):
    gain = 1.0
    for axis_at, parts in cuts:
        steps = jax.random.uniform(jax.random.fold_in(jax.random.fold_in(key, 6), axis_at), (parts,), jnp.float32, low / len(cuts), top_value / len(cuts))
        gain = gain * jnp.repeat(jnp.exp(steps), extent[axis_at] // parts).reshape((-1,) + (1,) * (len(extent) - 1 - axis_at))
    return gain


def noise(rng, shape, scale, limit, shards=(), kind=jnp.bfloat16):
    gain = steps_of(rng, shape, shards, -0.22, 0.18) if shards else 1.0
    entries = jax.random.normal(rng, shape, jnp.float32) * scale * gain
    return jnp.minimum(jnp.maximum(entries, -limit), limit).astype(kind)


def setup_inputs(seed: int = 0, part: int = 0) -> dict:
    key_of = jax.random.split(jax.random.key(seed), 7)
    part_keys = jax.random.split(jax.random.fold_in(key_of[6], part), 7)
    tokens = noise(part_keys[0], (TOKENS, D), 1.0, 6.0, ((0, 4),))
    gate_weight = noise(key_of[1], (EXPERTS, D, FF), D ** -0.5, 0.078125, ((2, 16),))
    up_weight = noise(key_of[2], (EXPERTS, D, FF), D ** -0.5, 0.078125, ((2, 16),))
    down_weight = noise(key_of[3], (EXPERTS, FF, D), FF ** -0.5, 0.046875, ((1, 4), (2, 4)))
    routes = draw_routes(jax.random.fold_in(jax.random.fold_in(key_of[6], part), 71), part)
    combine = jnp.clip(jax.random.uniform(part_keys[5], (TOKENS, 2), jnp.float32, 0.2, 1.0), 0.2, 1.0)
    return dict(tokens=tokens, gate_weight=gate_weight, up_weight=up_weight, down_weight=down_weight, routes=routes, combine=combine)


def reference(tokens, gate_weight, up_weight, down_weight, routes, combine):
    block = TOKENS // BLOCKS
    rows_route = jnp.repeat(routes, block, axis=0)
    mixed = jnp.zeros((TOKENS, D), jnp.float32)
    for expert in range(EXPERTS):
        coef = jnp.sum(combine * (rows_route == expert).astype(jnp.float32), axis=1)
        gate = jnp.dot(tokens, gate_weight[expert], preferred_element_type=jnp.float32)
        upward = jnp.dot(tokens, up_weight[expert], preferred_element_type=jnp.float32)
        hidden = (jax.nn.silu(gate) * upward).astype(jnp.bfloat16)
        part = jnp.dot(hidden, down_weight[expert], preferred_element_type=jnp.float32)
        mixed = mixed + coef[:, None] * part
    return mixed.astype(jnp.bfloat16)
```

```python
import functools

import jax
import jax.numpy as jnp
from jax import lax
from jax.experimental import pallas as pl
from jax.experimental.pallas import tpu as pltpu
from jax.sharding import PartitionSpec as P

F32 = jnp.float32
BF16 = jnp.bfloat16
VMEM_LIMIT = 40 * 1024 * 1024


def tile_of(size, most):
    tile = min(size, most)
    while size % tile:
        tile -= 128
    return tile


def params(grid_rank):
    return pltpu.CompilerParams(
        dimension_semantics=("arbitrary",) * grid_rank, vmem_limit_bytes=VMEM_LIMIT
    )


def gate_up_kernel(slot, parts, tk, info, *refs):
    own = refs[0]
    pieces = refs[1:1 + 3 * parts]
    gate_ref, up_ref, out_ref, held, gate_sum, up_sum, sems = refs[1 + 3 * parts:]
    step = pl.program_id(0)
    steps = pl.num_programs(0)
    block, wid, hid = info[slot, 0], info[8, 0], info[8, 1]
    per = held.shape[0] // parts
    width = per * tk
    away = jnp.bitwise_xor(block, wid)

    @pl.when(step == 0)
    def _():
        @pl.when(away == 0)
        def _():
            for q in range(parts * per):
                pltpu.make_async_copy(own.at[:, pl.ds(q * tk, tk)], held.at[q], sems.at[q]).start()

        for r in range(1, 4):
            @pl.when(away == r)
            def _(r=r):
                for j in range(parts):
                    base = jnp.bitwise_xor(hid, j) * per
                    for i in range(per):
                        pltpu.make_async_copy(
                            pieces[(r - 1) * parts + j].at[:, pl.ds(i * tk, tk)],
                            held.at[base + i],
                            sems.at[base + i],
                        ).start()

        gate_sum[...] = jnp.zeros_like(gate_sum)
        up_sum[...] = jnp.zeros_like(up_sum)

    pltpu.make_async_copy(own.at[:, pl.ds(0, tk)], held.at[step], sems.at[step]).wait()
    rows = held[step]
    gate_sum[...] += jnp.dot(rows, gate_ref[0], preferred_element_type=F32)
    up_sum[...] += jnp.dot(rows, up_ref[0], preferred_element_type=F32)

    @pl.when(step == steps - 1)
    def _():
        gate = gate_sum[...]
        out_ref[...] = (gate / (1.0 + jnp.exp(-gate)) * up_sum[...]).astype(out_ref.dtype)


def gate_up(slot, info, own, pieces, gate_weight, up_weight):
    _, width, units = gate_weight.shape
    rows = own.shape[0]
    parts = len(pieces) // 3
    tk = tile_of(width // parts, 512)
    steps = width // tk
    weight = pl.BlockSpec((1, tk, units), lambda k, info: (info[slot, 1], k, 0))
    anywhere = pl.BlockSpec(memory_space=pl.ANY)
    return pl.pallas_call(
        functools.partial(gate_up_kernel, slot, parts, tk),
        grid_spec=pltpu.PrefetchScalarGridSpec(
            num_scalar_prefetch=1,
            grid=(steps,),
            in_specs=[anywhere] * (1 + len(pieces)) + [weight, weight],
            out_specs=pl.BlockSpec((rows, units), lambda k, info: (0, 0)),
            scratch_shapes=[
                pltpu.VMEM((steps, rows, tk), BF16),
                pltpu.VMEM((rows, units), F32),
                pltpu.VMEM((rows, units), F32),
                pltpu.SemaphoreType.DMA((steps,)),
            ],
        ),
        out_shape=jax.ShapeDtypeStruct((rows, units), BF16),
        compiler_params=params(1),
        cost_estimate=pl.CostEstimate(
            flops=4 * rows * width * units,
            bytes_accessed=4 * width * units,
            transcendentals=rows * units,
        ),
        name="gate_up",
    )(info, own, *pieces, gate_weight, up_weight)


def down_kernel(slot, info, own, near, far, middle, end, coef_ref, weight_ref, old_ref, out_ref, held, total, sems):
    step = pl.program_id(0)
    steps = pl.num_programs(0)
    wid = info[8, 0]
    inner = (wid == 1) | (wid == 2)

    @pl.when(step == 0)
    def _():
        for r, ref in enumerate((own, near, far)):
            pltpu.make_async_copy(ref, held.at[r], sems.at[r]).start()

        @pl.when(inner)
        def _():
            pltpu.make_async_copy(middle, held.at[3], sems.at[3]).start()

        @pl.when(jnp.logical_not(inner))
        def _():
            pltpu.make_async_copy(end, held.at[3], sems.at[3]).start()

        total[...] = jnp.zeros_like(total)

    pltpu.make_async_copy(own, held.at[step], sems.at[step]).wait()
    total[...] += jnp.dot(held[step], weight_ref[0], preferred_element_type=F32)

    @pl.when(step == steps - 1)
    def _():
        part = coef_ref[0] * total[...]
        first = info[slot, 2] == 1

        @pl.when(first)
        def _():
            out_ref[0] = part

        @pl.when(jnp.logical_not(first))
        def _():
            out_ref[0] = old_ref[0] + part


def down(slot, info, shards, coef, down_weight, sums):
    rows, units = shards[0].shape
    width = down_weight.shape[2]
    anywhere = pl.BlockSpec(memory_space=pl.ANY)
    here = pl.BlockSpec((1, rows, width), lambda k, info: (info[slot, 0], 0, 0))
    return pl.pallas_call(
        functools.partial(down_kernel, slot),
        grid_spec=pltpu.PrefetchScalarGridSpec(
            num_scalar_prefetch=1,
            grid=(4,),
            in_specs=[anywhere] * 5 + [
                pl.BlockSpec((1, rows, 1), lambda k, info: (info[slot, 3], 0, 0)),
                pl.BlockSpec(
                    (1, units, width),
                    lambda k, info: (info[slot, 1], jnp.bitwise_xor(info[8, 0], k), 0),
                ),
                here,
            ],
            out_specs=here,
            scratch_shapes=[
                pltpu.VMEM((4, rows, units), BF16),
                pltpu.VMEM((rows, width), F32),
                pltpu.SemaphoreType.DMA((4,)),
            ],
        ),
        out_shape=jax.ShapeDtypeStruct(sums.shape, F32),
        input_output_aliases={8: 0},
        compiler_params=params(1),
        cost_estimate=pl.CostEstimate(
            flops=8 * rows * units * width, bytes_accessed=8 * units * width, transcendentals=0
        ),
        name="down",
    )(info, *shards, coef, down_weight, sums)


FAR = [(0, 2), (2, 0), (1, 3), (3, 1)]
NEAR = [(0, 1), (1, 0), (2, 3), (3, 2)]
MIDDLE = [(1, 2), (2, 1)]
OUTWARD = [(1, 0), (2, 3)]
ACROSS = [(0, 2), (2, 0), (1, 3), (3, 1)]
TWIN = [(0, 1), (1, 0), (2, 3), (3, 2)]


def sparse_device(tokens, gate_weight, up_weight, down_weight, routes, combine):
    experts = gate_weight.shape[0]
    blocks = routes.shape[0]
    rows = combine.shape[0] // blocks
    wid = lax.axis_index("wid")
    hid = lax.axis_index("hid")
    inner = (wid == 1) | (wid == 2)

    labels = jnp.arange(experts, dtype=jnp.int32)
    picked = routes[:, :, None] == labels[None, None, :]
    coef = jnp.sum(combine.reshape(blocks, rows, -1)[:, :, :, None] * picked.astype(F32)[:, None], axis=2)
    coef = jnp.transpose(coef, (0, 2, 1)).reshape(blocks * experts, rows, 1)
    named = jnp.any(picked, axis=1)
    flat = named.reshape(-1).astype(jnp.int32)
    place = jnp.cumsum(flat) - 1
    count = jnp.sum(flat)
    number = jnp.arange(blocks * experts, dtype=jnp.int32)
    hit = (place[None, :] == number[:, None]) & (flat[None, :] == 1)
    pair = jnp.sum(jnp.where(hit, number[None, :], 0), axis=1)
    block_of = pair // experts
    before = jnp.concatenate([jnp.full((1,), -1, jnp.int32), block_of[:-1]])
    info = jnp.stack([block_of, pair % experts, (block_of != before).astype(jnp.int32), pair], axis=1)
    here = jnp.stack([wid, hid, wid, hid]).astype(jnp.int32)[None]
    info = jnp.concatenate([info, here], axis=0)

    quarter = tokens.shape[1] // 4
    mine = lax.dynamic_slice_in_dim(tokens, hid * quarter, quarter, axis=1)
    far = lax.ppermute(mine, "wid", FAR)
    near = lax.ppermute(mine, "wid", NEAR)
    middle = lax.ppermute(mine, "wid", MIDDLE)
    outer = lax.ppermute(far, "wid", OUTWARD)
    last = jnp.where(inner, middle, outer)
    pieces = []
    for piece in (near, far, last):
        across = lax.ppermute(piece, "hid", ACROSS)
        twin = lax.ppermute(piece, "hid", TWIN)
        diagonal = lax.ppermute(across, "hid", TWIN)
        pieces += [piece, twin, across, diagonal]

    def branch(slots):
        def run(info, coef, sums, *pieces):
            waiting = []
            for slot in range(slots):
                hidden = gate_up(slot, info, tokens, pieces, gate_weight, up_weight)
                far = lax.ppermute(hidden, "wid", FAR)
                near = lax.ppermute(hidden, "wid", NEAR)
                middle = lax.ppermute(hidden, "wid", MIDDLE)
                outer = lax.ppermute(far, "wid", OUTWARD)
                waiting.append((hidden, near, far, middle, outer))
            for slot in range(slots):
                sums = down(slot, info, waiting[slot], coef, down_weight, sums)
            return sums

        return run

    sums = jnp.zeros((blocks, rows, down_weight.shape[2]), F32)
    sums = lax.switch(count - 1, [branch(n + 1) for n in range(blocks * experts)], info, coef, sums, *pieces)

    core, x = hid % 2, hid // 2
    pairs = sums.reshape(2, 2, rows, -1)
    to_twin = lax.dynamic_index_in_dim(pairs, 1 - core, axis=1, keepdims=False).astype(BF16)
    kept = lax.dynamic_index_in_dim(pairs, core, axis=1, keepdims=False)
    kept = kept + lax.ppermute(to_twin, "hid", TWIN).astype(F32)
    to_across = lax.dynamic_index_in_dim(kept, 1 - x, axis=0, keepdims=False).astype(BF16)
    own = lax.dynamic_index_in_dim(kept, x, axis=0, keepdims=False)
    return (own + lax.ppermute(to_across, "hid", ACROSS).astype(F32)).astype(BF16)


def dense_device(tokens, gate_weight, up_weight, down_weight, routes, combine):
    experts = gate_weight.shape[0]
    block = combine.shape[0] // routes.shape[0]
    rows_route = jnp.repeat(routes, block, axis=0)
    labels = jnp.arange(experts, dtype=jnp.int32)
    picked = (rows_route[:, :, None] == labels[None, None, :]).astype(F32)
    weights = jnp.sum(combine[:, :, None] * picked, axis=1)
    piece = lax.all_gather(tokens, "wid", axis=0, tiled=True)
    gate = jnp.einsum("td,edf->etf", piece, gate_weight, preferred_element_type=F32)
    upward = jnp.einsum("td,edf->etf", piece, up_weight, preferred_element_type=F32)
    hidden = (jax.nn.silu(gate) * upward).astype(BF16)
    summed = jnp.einsum(
        "etf,efd->etd",
        lax.all_gather(hidden, "wid", axis=2, tiled=True),
        down_weight,
        preferred_element_type=F32,
    )
    partial_value = jnp.sum(jnp.transpose(weights)[:, :, None] * summed, axis=0)
    own_rows = lax.psum_scatter(partial_value, "hid", scatter_dimension=0, tiled=True)
    return own_rows.astype(BF16)


def solution(mesh):
    placed = (
        P(("grp", "wid"), None),
        P(None, None, ("hid", "wid")),
        P(None, None, ("hid", "wid")),
        P(None, "hid", "wid"),
        P("grp", None),
        P("grp", None),
    )

    def program(tokens, gate_weight, up_weight, down_weight, routes, combine):
        blocks = routes.shape[0] // mesh.shape["grp"]
        square = mesh.shape["wid"] == 4 and mesh.shape["hid"] == 4 and blocks == 4
        return jax.shard_map(
            sparse_device if square else dense_device,
            mesh=mesh,
            in_specs=placed,
            out_specs=P(("grp", "hid"), "wid"),
            check_vma=False,
        )(tokens, gate_weight, up_weight, down_weight, routes, combine)

    return program
```

```python
import functools

import jax
import jax.numpy as jnp
from jax import lax
from jax.experimental import pallas as pl
from jax.experimental.pallas import tpu as pltpu
from jax.sharding import PartitionSpec as P

F32 = jnp.float32
BF16 = jnp.bfloat16
VMEM_LIMIT = 40 * 1024 * 1024


def tile_of(size, most):
    tile = min(size, most)
    while size % tile:
        tile -= 128
    return tile


def params(grid_rank):
    return pltpu.CompilerParams(
        dimension_semantics=("arbitrary",) * grid_rank, vmem_limit_bytes=VMEM_LIMIT
    )


def gate_up_kernel(slot, parts, info, *refs):
    own = refs[0]
    pieces = refs[1:1 + 3 * parts]
    gate_ref, up_ref, out_ref, held, gate_held, up_held, gate_sum, up_sum, sems, gate_sems, up_sems = refs[1 + 3 * parts:]
    steps, _, tk = held.shape
    per = steps // parts
    block, expert, wid, hid = info[slot, 0], info[slot, 1], info[8, 0], info[8, 1]
    away = jnp.bitwise_xor(block, wid)

    @pl.when(away == 0)
    def _():
        for q in range(steps):
            pltpu.make_async_copy(own.at[:, pl.ds(q * tk, tk)], held.at[q], sems.at[q]).start()

    for r in range(1, 4):
        @pl.when(away == r)
        def _(r=r):
            for j in range(parts):
                base = jnp.bitwise_xor(hid, j) * per
                for i in range(per):
                    pltpu.make_async_copy(
                        pieces[(r - 1) * parts + j].at[:, pl.ds(i * tk, tk)],
                        held.at[base + i],
                        sems.at[base + i],
                    ).start()

    def copies(k):
        rows = pl.ds(k * tk, tk)
        return (
            pltpu.make_async_copy(gate_ref.at[expert, rows], gate_held.at[k], gate_sems.at[k]),
            pltpu.make_async_copy(up_ref.at[expert, rows], up_held.at[k], up_sems.at[k]),
        )

    for k in range(steps):
        for copy in copies(k):
            copy.start()
    gate_sum[...] = jnp.zeros_like(gate_sum)
    up_sum[...] = jnp.zeros_like(up_sum)

    @pl.loop(0, steps)
    def _(k):
        pltpu.make_async_copy(own.at[:, pl.ds(0, tk)], held.at[k], sems.at[k]).wait()
        for copy in copies(k):
            copy.wait()
        rows = held[k]
        gate_sum[...] += jnp.dot(rows, gate_held[k], preferred_element_type=F32)
        up_sum[...] += jnp.dot(rows, up_held[k], preferred_element_type=F32)

    gate = gate_sum[...]
    out_ref[...] = (gate / (1.0 + jnp.exp(-gate)) * up_sum[...]).astype(out_ref.dtype)


def gate_up(slot, info, own, pieces, gate_weight, up_weight):
    _, width, units = gate_weight.shape
    rows = own.shape[0]
    parts = len(pieces) // 3
    tk = tile_of(width // parts, 768)
    steps = width // tk
    anywhere = pl.BlockSpec(memory_space=pl.ANY)
    return pl.pallas_call(
        functools.partial(gate_up_kernel, slot, parts),
        grid_spec=pltpu.PrefetchScalarGridSpec(
            num_scalar_prefetch=1,
            grid=(1,),
            in_specs=[anywhere] * (3 + len(pieces)),
            out_specs=pl.BlockSpec((rows, units), lambda k, info: (0, 0)),
            scratch_shapes=[
                pltpu.VMEM((steps, rows, tk), BF16),
                pltpu.VMEM((steps, tk, units), BF16),
                pltpu.VMEM((steps, tk, units), BF16),
                pltpu.VMEM((rows, units), F32),
                pltpu.VMEM((rows, units), F32),
                pltpu.SemaphoreType.DMA((steps,)),
                pltpu.SemaphoreType.DMA((steps,)),
                pltpu.SemaphoreType.DMA((steps,)),
            ],
        ),
        out_shape=jax.ShapeDtypeStruct((rows, units), BF16),
        compiler_params=params(1),
        cost_estimate=pl.CostEstimate(
            flops=4 * rows * width * units,
            bytes_accessed=4 * width * units,
            transcendentals=rows * units,
        ),
        name="gate_up",
    )(info, own, *pieces, gate_weight, up_weight)


def down_kernel(slot, info, own, near, far, middle, end, weight_ref, coef_ref, old_ref, out_ref, held, weight_held, sems, weight_sems):
    wid, expert = info[8, 0], info[slot, 1]
    inner = (wid == 1) | (wid == 2)
    steps, rows, tk = held.shape
    per = steps // 4

    def start(ref, r):
        for i in range(per):
            pltpu.make_async_copy(ref.at[:, pl.ds(i * tk, tk)], held.at[r * per + i], sems.at[r * per + i]).start()

    for r, ref in enumerate((own, near, far)):
        start(ref, r)

    @pl.when(inner)
    def _():
        start(middle, 3)

    @pl.when(jnp.logical_not(inner))
    def _():
        start(end, 3)

    def weight_copy(k):
        origin = jnp.bitwise_xor(wid, k // per) * per + k % per
        return pltpu.make_async_copy(
            weight_ref.at[expert, pl.ds(origin * tk, tk)], weight_held.at[k], weight_sems.at[k]
        )

    for k in range(steps):
        weight_copy(k).start()
    for k in range(steps):
        pltpu.make_async_copy(own.at[:, pl.ds(0, tk)], held.at[k], sems.at[k]).wait()
        weight_copy(k).wait()
        if k == 0:
            out_ref[0] = jnp.dot(held[k], weight_held[k], preferred_element_type=F32)
        else:
            out_ref[0] += jnp.dot(held[k], weight_held[k], preferred_element_type=F32)
    first = info[slot, 2] == 1

    @pl.when(first)
    def _():
        out_ref[0] = coef_ref[0] * out_ref[0]

    @pl.when(jnp.logical_not(first))
    def _():
        out_ref[0] = old_ref[0] + coef_ref[0] * out_ref[0]


def down(slot, info, shards, coef, down_weight, sums):
    rows, units = shards[0].shape
    width = down_weight.shape[2]
    tk = tile_of(units, 1024)
    steps = 4 * units // tk
    anywhere = pl.BlockSpec(memory_space=pl.ANY)
    here = pl.BlockSpec((1, rows, width), lambda k, info: (info[slot, 0], 0, 0))
    return pl.pallas_call(
        functools.partial(down_kernel, slot),
        grid_spec=pltpu.PrefetchScalarGridSpec(
            num_scalar_prefetch=1,
            grid=(1,),
            in_specs=[anywhere] * 6 + [
                pl.BlockSpec((1, rows, 1), lambda k, info: (info[slot, 3], 0, 0)),
                here,
            ],
            out_specs=here,
            scratch_shapes=[
                pltpu.VMEM((steps, rows, tk), BF16),
                pltpu.VMEM((steps, tk, width), BF16),
                pltpu.SemaphoreType.DMA((steps,)),
                pltpu.SemaphoreType.DMA((steps,)),
            ],
        ),
        out_shape=jax.ShapeDtypeStruct(sums.shape, F32),
        input_output_aliases={8: 0},
        compiler_params=params(1),
        cost_estimate=pl.CostEstimate(
            flops=8 * rows * units * width, bytes_accessed=8 * units * width, transcendentals=0
        ),
        name="down",
    )(info, *shards, down_weight, coef, sums)


FAR = [(0, 2), (2, 0), (1, 3), (3, 1)]
NEAR = [(0, 1), (1, 0), (2, 3), (3, 2)]
MIDDLE = [(1, 2), (2, 1)]
OUTWARD = [(1, 0), (2, 3)]
ACROSS = [(0, 2), (2, 0), (1, 3), (3, 1)]
TWIN = [(0, 1), (1, 0), (2, 3), (3, 2)]


def sparse_device(tokens, gate_weight, up_weight, down_weight, routes, combine):
    experts = gate_weight.shape[0]
    blocks = routes.shape[0]
    rows = combine.shape[0] // blocks
    wid = lax.axis_index("wid")
    hid = lax.axis_index("hid")
    inner = (wid == 1) | (wid == 2)

    labels = jnp.arange(experts, dtype=jnp.int32)
    picked = routes[:, :, None] == labels[None, None, :]
    coef = jnp.sum(combine.reshape(blocks, rows, -1)[:, :, :, None] * picked.astype(F32)[:, None], axis=2)
    coef = jnp.transpose(coef, (0, 2, 1)).reshape(blocks * experts, rows, 1)
    named = jnp.any(picked, axis=1)
    flat = named.reshape(-1).astype(jnp.int32)
    place = jnp.cumsum(flat) - 1
    count = jnp.sum(flat)
    number = jnp.arange(blocks * experts, dtype=jnp.int32)
    hit = (place[None, :] == number[:, None]) & (flat[None, :] == 1)
    pair = jnp.sum(jnp.where(hit, number[None, :], 0), axis=1)
    block_of = pair // experts
    before = jnp.concatenate([jnp.full((1,), -1, jnp.int32), block_of[:-1]])
    info = jnp.stack([block_of, pair % experts, (block_of != before).astype(jnp.int32), pair], axis=1)
    here = jnp.stack([wid, hid, wid, hid]).astype(jnp.int32)[None]
    info = jnp.concatenate([info, here], axis=0)

    quarter = tokens.shape[1] // 4
    mine = lax.dynamic_slice_in_dim(tokens, hid * quarter, quarter, axis=1)
    far = lax.ppermute(mine, "wid", FAR)
    near = lax.ppermute(mine, "wid", NEAR)
    middle = lax.ppermute(mine, "wid", MIDDLE)
    outer = lax.ppermute(far, "wid", OUTWARD)
    last = jnp.where(inner, middle, outer)
    pieces = []
    for piece in (near, far, last):
        across = lax.ppermute(piece, "hid", ACROSS)
        twin = lax.ppermute(piece, "hid", TWIN)
        diagonal = lax.ppermute(across, "hid", TWIN)
        pieces += [piece, twin, across, diagonal]

    def exchange(hidden):
        far = lax.ppermute(hidden, "wid", FAR)
        near = lax.ppermute(hidden, "wid", NEAR)
        middle = lax.ppermute(hidden, "wid", MIDDLE)
        outer = lax.ppermute(far, "wid", OUTWARD)
        return hidden, near, far, middle, outer

    def branch(slots):
        def run(info, coef, sums, *pieces):
            sent = None
            for slot in range(slots):
                hidden = gate_up(slot, info, tokens, pieces, gate_weight, up_weight)
                if sent is not None:
                    sums = down(slot - 1, info, sent, coef, down_weight, sums)
                sent = exchange(hidden)
            return down(slots - 1, info, sent, coef, down_weight, sums)

        return run

    most = 4
    sums = jnp.zeros((blocks, rows, down_weight.shape[2]), F32)
    sums = lax.switch(
        jnp.minimum(count, most) - 1, [branch(n + 1) for n in range(most)], info, coef, sums, *pieces
    )

    def further(state):
        at, sums = state
        one = jnp.concatenate([lax.dynamic_slice_in_dim(info, at, 1, axis=0), info[1:]], axis=0)
        sent = exchange(gate_up(0, one, tokens, pieces, gate_weight, up_weight))
        return at + 1, down(0, one, sent, coef, down_weight, sums)

    _, sums = lax.while_loop(lambda state: state[0] < count, further, (jnp.int32(most), sums))

    core, x = hid % 2, hid // 2
    pairs = sums.reshape(2, 2, rows, -1)
    to_twin = lax.dynamic_index_in_dim(pairs, 1 - core, axis=1, keepdims=False).astype(BF16)
    kept = lax.dynamic_index_in_dim(pairs, core, axis=1, keepdims=False)
    kept = kept + lax.ppermute(to_twin, "hid", TWIN).astype(F32)
    to_across = lax.dynamic_index_in_dim(kept, 1 - x, axis=0, keepdims=False).astype(BF16)
    own = lax.dynamic_index_in_dim(kept, x, axis=0, keepdims=False)
    return (own + lax.ppermute(to_across, "hid", ACROSS).astype(F32)).astype(BF16)


def dense_device(tokens, gate_weight, up_weight, down_weight, routes, combine):
    experts = gate_weight.shape[0]
    block = combine.shape[0] // routes.shape[0]
    rows_route = jnp.repeat(routes, block, axis=0)
    labels = jnp.arange(experts, dtype=jnp.int32)
    picked = (rows_route[:, :, None] == labels[None, None, :]).astype(F32)
    weights = jnp.sum(combine[:, :, None] * picked, axis=1)
    piece = lax.all_gather(tokens, "wid", axis=0, tiled=True)
    gate = jnp.einsum("td,edf->etf", piece, gate_weight, preferred_element_type=F32)
    upward = jnp.einsum("td,edf->etf", piece, up_weight, preferred_element_type=F32)
    hidden = (jax.nn.silu(gate) * upward).astype(BF16)
    summed = jnp.einsum(
        "etf,efd->etd",
        lax.all_gather(hidden, "wid", axis=2, tiled=True),
        down_weight,
        preferred_element_type=F32,
    )
    partial_value = jnp.sum(jnp.transpose(weights)[:, :, None] * summed, axis=0)
    own_rows = lax.psum_scatter(partial_value, "hid", scatter_dimension=0, tiled=True)
    return own_rows.astype(BF16)


def solution(mesh):
    placed = (
        P(("grp", "wid"), None),
        P(None, None, ("hid", "wid")),
        P(None, None, ("hid", "wid")),
        P(None, "hid", "wid"),
        P("grp", None),
        P("grp", None),
    )

    def program(tokens, gate_weight, up_weight, down_weight, routes, combine):
        blocks = routes.shape[0] // mesh.shape["grp"]
        square = mesh.shape["wid"] == 4 and mesh.shape["hid"] == 4 and blocks == 4
        return jax.shard_map(
            sparse_device if square else dense_device,
            mesh=mesh,
            in_specs=placed,
            out_specs=P(("grp", "hid"), "wid"),
            check_vma=False,
        )(tokens, gate_weight, up_weight, down_weight, routes, combine)

    return program
```

```python
import functools

import jax
import jax.numpy as jnp
from jax import lax
from jax.experimental import pallas as pl
from jax.experimental.pallas import tpu as pltpu
from jax.sharding import PartitionSpec as P

F32 = jnp.float32
BF16 = jnp.bfloat16
VMEM_LIMIT = 40 * 1024 * 1024


def tile_of(size, most):
    tile = min(size, most)
    while size % tile:
        tile -= 128
    return tile


def params(grid_rank):
    return pltpu.CompilerParams(
        dimension_semantics=("arbitrary",) * grid_rank, vmem_limit_bytes=VMEM_LIMIT
    )


def gate_up_kernel(slot, parts, info, *refs):
    own = refs[0]
    pieces = refs[1:1 + 3 * parts]
    gate_ref, up_ref, out_ref, held, gate_held, up_held, sems, gate_sems, up_sems = refs[1 + 3 * parts:]
    chunks, halves, depth, columns = gate_held.shape
    part = held.shape[1] // parts
    block, expert, wid, hid = info[slot, 0], info[slot, 1], info[8, 0], info[8, 1]
    away = jnp.bitwise_xor(block, wid)

    @pl.when(away == 0)
    def _():
        for q in range(parts):
            here = pl.ds(q * part, part)
            pltpu.make_async_copy(own.at[:, here], held.at[:, here], sems.at[q]).start()

    for r in range(1, 4):
        @pl.when(away == r)
        def _(r=r):
            for j in range(parts):
                q = jnp.bitwise_xor(hid, j)
                here = pl.ds(pl.multiple_of(q * part, 128), part)
                pltpu.make_async_copy(pieces[(r - 1) * parts + j], held.at[:, here], sems.at[q]).start()

    def copies(n, half):
        rows = pl.ds(half * depth, depth)
        there = pl.ds(pl.multiple_of(n * columns, 128), columns)
        return (
            pltpu.make_async_copy(gate_ref.at[expert, rows, there], gate_held.at[n, half], gate_sems.at[n, half]),
            pltpu.make_async_copy(up_ref.at[expert, rows, there], up_held.at[n, half], up_sems.at[n, half]),
        )

    for n in range(chunks):
        for half in range(halves):
            for copy in copies(n, half):
                copy.start()
    for q in range(parts):
        here = pl.ds(q * part, part)
        pltpu.make_async_copy(own.at[:, here], held.at[:, here], sems.at[q]).wait()

    @pl.loop(0, chunks)
    def _(n):
        gate = up = None
        for half in range(halves):
            for copy in copies(n, half):
                copy.wait()
            rows = held[:, half * depth:(half + 1) * depth]
            more_gate = jnp.dot(rows, gate_held[n, half], preferred_element_type=F32)
            more_up = jnp.dot(rows, up_held[n, half], preferred_element_type=F32)
            gate = more_gate if gate is None else gate + more_gate
            up = more_up if up is None else up + more_up
        there = pl.ds(pl.multiple_of(n * columns, 128), columns)
        out_ref[:, there] = (gate / (1.0 + jnp.exp(-gate)) * up).astype(out_ref.dtype)


def gate_up(slot, info, own, pieces, gate_weight, up_weight):
    _, width, units = gate_weight.shape
    rows = own.shape[0]
    parts = len(pieces) // 3
    columns = tile_of(units, 256)
    held = pltpu.VMEM((units // columns, 2, width // 2, columns), BF16)
    arrived = pltpu.SemaphoreType.DMA((units // columns, 2))
    anywhere = pl.BlockSpec(memory_space=pl.ANY)
    return pl.pallas_call(
        functools.partial(gate_up_kernel, slot, parts),
        grid_spec=pltpu.PrefetchScalarGridSpec(
            num_scalar_prefetch=1,
            grid=(1,),
            in_specs=[anywhere] * (3 + len(pieces)),
            out_specs=pl.BlockSpec((rows, units), lambda k, info: (0, 0)),
            scratch_shapes=[
                pltpu.VMEM((rows, width), BF16),
                held,
                held,
                pltpu.SemaphoreType.DMA((parts,)),
                arrived,
                arrived,
            ],
        ),
        out_shape=jax.ShapeDtypeStruct((rows, units), BF16),
        compiler_params=params(1),
        cost_estimate=pl.CostEstimate(
            flops=4 * rows * width * units,
            bytes_accessed=4 * width * units,
            transcendentals=rows * units,
        ),
        name="gate_up",
    )(info, own, *pieces, gate_weight, up_weight)


def down_kernel(slot, info, own, near, far, middle, end, weight_ref, coef_ref, old_ref, out_ref, held, weight_held, sems, weight_sems):
    wid, expert = info[8, 0], info[slot, 1]
    inner = (wid == 1) | (wid == 2)
    chunks, _, columns = weight_held.shape
    units = held.shape[1] // 4

    def place(r):
        return pl.ds(pl.multiple_of(jnp.bitwise_xor(wid, r) * units, 128), units)

    for r, ref in enumerate((own, near, far)):
        pltpu.make_async_copy(ref, held.at[:, place(r)], sems.at[r]).start()

    @pl.when(inner)
    def _():
        pltpu.make_async_copy(middle, held.at[:, place(3)], sems.at[3]).start()

    @pl.when(jnp.logical_not(inner))
    def _():
        pltpu.make_async_copy(end, held.at[:, place(3)], sems.at[3]).start()

    def weight_copy(n):
        there = pl.ds(pl.multiple_of(n * columns, 128), columns)
        return pltpu.make_async_copy(weight_ref.at[expert, :, there], weight_held.at[n], weight_sems.at[n])

    for n in range(chunks):
        weight_copy(n).start()
    for r in range(4):
        pltpu.make_async_copy(own, held.at[:, place(r)], sems.at[r]).wait()
    carried = jnp.where(info[slot, 2] == 1, 0.0, 1.0)

    @pl.loop(0, chunks)
    def _(n):
        weight_copy(n).wait()
        there = pl.ds(pl.multiple_of(n * columns, 128), columns)
        part = jnp.dot(held[...], weight_held[n], preferred_element_type=F32)
        out_ref[0, :, there] = carried * old_ref[0, :, there] + coef_ref[0] * part


def down(slot, info, shards, coef, down_weight, sums):
    rows, units = shards[0].shape
    width = down_weight.shape[2]
    columns = tile_of(width, 256)
    anywhere = pl.BlockSpec(memory_space=pl.ANY)
    here = pl.BlockSpec((1, rows, width), lambda k, info: (info[slot, 0], 0, 0))
    return pl.pallas_call(
        functools.partial(down_kernel, slot),
        grid_spec=pltpu.PrefetchScalarGridSpec(
            num_scalar_prefetch=1,
            grid=(1,),
            in_specs=[anywhere] * 6 + [
                pl.BlockSpec((1, rows, 1), lambda k, info: (info[slot, 3], 0, 0)),
                here,
            ],
            out_specs=here,
            scratch_shapes=[
                pltpu.VMEM((rows, 4 * units), BF16),
                pltpu.VMEM((width // columns, 4 * units, columns), BF16),
                pltpu.SemaphoreType.DMA((4,)),
                pltpu.SemaphoreType.DMA((width // columns,)),
            ],
        ),
        out_shape=jax.ShapeDtypeStruct(sums.shape, F32),
        input_output_aliases={8: 0},
        compiler_params=params(1),
        cost_estimate=pl.CostEstimate(
            flops=8 * rows * units * width, bytes_accessed=8 * units * width, transcendentals=0
        ),
        name="down",
    )(info, *shards, down_weight, coef, sums)


FAR = [(0, 2), (2, 0), (1, 3), (3, 1)]
NEAR = [(0, 1), (1, 0), (2, 3), (3, 2)]
MIDDLE = [(1, 2), (2, 1)]
OUTWARD = [(1, 0), (2, 3)]
ACROSS = [(0, 2), (2, 0), (1, 3), (3, 1)]
TWIN = [(0, 1), (1, 0), (2, 3), (3, 2)]


def sparse_device(tokens, gate_weight, up_weight, down_weight, routes, combine):
    experts = gate_weight.shape[0]
    blocks = routes.shape[0]
    rows = combine.shape[0] // blocks
    wid = lax.axis_index("wid")
    hid = lax.axis_index("hid")
    inner = (wid == 1) | (wid == 2)

    labels = jnp.arange(experts, dtype=jnp.int32)
    picked = routes[:, :, None] == labels[None, None, :]
    coef = jnp.sum(combine.reshape(blocks, rows, -1)[:, :, :, None] * picked.astype(F32)[:, None], axis=2)
    coef = jnp.transpose(coef, (0, 2, 1)).reshape(blocks * experts, rows, 1)
    named = jnp.any(picked, axis=1)
    flat = named.reshape(-1).astype(jnp.int32)
    place = jnp.cumsum(flat) - 1
    count = jnp.sum(flat)
    number = jnp.arange(blocks * experts, dtype=jnp.int32)
    hit = (place[None, :] == number[:, None]) & (flat[None, :] == 1)
    pair = jnp.sum(jnp.where(hit, number[None, :], 0), axis=1)
    block_of = pair // experts
    before = jnp.concatenate([jnp.full((1,), -1, jnp.int32), block_of[:-1]])
    info = jnp.stack([block_of, pair % experts, (block_of != before).astype(jnp.int32), pair], axis=1)
    here = jnp.stack([wid, hid, wid, hid]).astype(jnp.int32)[None]
    info = jnp.concatenate([info, here], axis=0)

    quarter = tokens.shape[1] // 4
    mine = lax.dynamic_slice_in_dim(tokens, hid * quarter, quarter, axis=1)
    far = lax.ppermute(mine, "wid", FAR)
    near = lax.ppermute(mine, "wid", NEAR)
    middle = lax.ppermute(mine, "wid", MIDDLE)
    outer = lax.ppermute(far, "wid", OUTWARD)
    last = jnp.where(inner, middle, outer)
    pieces = []
    for piece in (near, far, last):
        across = lax.ppermute(piece, "hid", ACROSS)
        twin = lax.ppermute(piece, "hid", TWIN)
        diagonal = lax.ppermute(across, "hid", TWIN)
        pieces += [piece, twin, across, diagonal]

    def after(value, *done):
        return lax.optimization_barrier((value, *done))[0]

    def outward(hidden, near, far):
        middle = lax.ppermute(after(hidden, far), "wid", MIDDLE)
        outer = lax.ppermute(far, "wid", OUTWARD)
        return hidden, near, far, middle, outer

    def inward(hidden):
        return hidden, lax.ppermute(hidden, "wid", NEAR), lax.ppermute(hidden, "wid", FAR)

    def branch(slots):
        def run(info, coef, sums, *pieces):
            first, second = [], []
            for slot in range(slots + 1):
                if slot < slots:
                    ready = info if slot < 2 else after(info, first[slot - 2][2])
                    first.append(inward(gate_up(slot, ready, tokens, pieces, gate_weight, up_weight)))
                if slot >= 2:
                    ready = info if slot >= slots else after(info, first[slot][0])
                    sums = down(slot - 2, ready, second[slot - 2], coef, down_weight, sums)
                if slot >= 1:
                    hidden, near, far = first[slot - 1]
                    far = far if slot < 2 else after(far, sums)
                    second.append(outward(hidden, near, far))
            return down(slots - 1, info, second[slots - 1], coef, down_weight, sums)

        return run

    most = 4
    sums = jnp.full((blocks, rows, down_weight.shape[2]), jnp.where(count < 0, 1.0, 0.0).astype(F32))
    sums = lax.switch(
        jnp.minimum(count, most) - 1, [branch(n + 1) for n in range(most)], info, coef, sums, *pieces
    )

    def further(state):
        at, sums = state
        one = jnp.concatenate([lax.dynamic_slice_in_dim(info, at, 1, axis=0), info[1:]], axis=0)
        sent = outward(*inward(gate_up(0, one, tokens, pieces, gate_weight, up_weight)))
        return at + 1, down(0, one, sent, coef, down_weight, sums)

    _, sums = lax.while_loop(lambda state: state[0] < count, further, (jnp.int32(most), sums))

    core, x = hid % 2, hid // 2
    pairs = sums.reshape(2, 2, rows, -1)
    to_twin = lax.dynamic_index_in_dim(pairs, 1 - core, axis=1, keepdims=False).astype(BF16)
    kept = lax.dynamic_index_in_dim(pairs, core, axis=1, keepdims=False)
    kept = kept + lax.ppermute(to_twin, "hid", TWIN).astype(F32)
    to_across = lax.dynamic_index_in_dim(kept, 1 - x, axis=0, keepdims=False).astype(BF16)
    own = lax.dynamic_index_in_dim(kept, x, axis=0, keepdims=False)
    return (own + lax.ppermute(to_across, "hid", ACROSS).astype(F32)).astype(BF16)


def dense_device(tokens, gate_weight, up_weight, down_weight, routes, combine):
    experts = gate_weight.shape[0]
    block = combine.shape[0] // routes.shape[0]
    rows_route = jnp.repeat(routes, block, axis=0)
    labels = jnp.arange(experts, dtype=jnp.int32)
    picked = (rows_route[:, :, None] == labels[None, None, :]).astype(F32)
    weights = jnp.sum(combine[:, :, None] * picked, axis=1)
    piece = lax.all_gather(tokens, "wid", axis=0, tiled=True)
    gate = jnp.einsum("td,edf->etf", piece, gate_weight, preferred_element_type=F32)
    upward = jnp.einsum("td,edf->etf", piece, up_weight, preferred_element_type=F32)
    hidden = (jax.nn.silu(gate) * upward).astype(BF16)
    summed = jnp.einsum(
        "etf,efd->etd",
        lax.all_gather(hidden, "wid", axis=2, tiled=True),
        down_weight,
        preferred_element_type=F32,
    )
    partial_value = jnp.sum(jnp.transpose(weights)[:, :, None] * summed, axis=0)
    own_rows = lax.psum_scatter(partial_value, "hid", scatter_dimension=0, tiled=True)
    return own_rows.astype(BF16)


def solution(mesh):
    placed = (
        P(("grp", "wid"), None),
        P(None, None, ("hid", "wid")),
        P(None, None, ("hid", "wid")),
        P(None, "hid", "wid"),
        P("grp", None),
        P("grp", None),
    )

    def program(tokens, gate_weight, up_weight, down_weight, routes, combine):
        blocks = routes.shape[0] // mesh.shape["grp"]
        square = mesh.shape["wid"] == 4 and mesh.shape["hid"] == 4 and blocks == 4
        return jax.shard_map(
            sparse_device if square else dense_device,
            mesh=mesh,
            in_specs=placed,
            out_specs=P(("grp", "hid"), "wid"),
            check_vma=False,
        )(tokens, gate_weight, up_weight, down_weight, routes, combine)

    return program
```

```python
import functools

import jax
import jax.numpy as jnp
from jax import lax
from jax.experimental import pallas as pl
from jax.experimental.pallas import tpu as pltpu
from jax.sharding import PartitionSpec as P

F32 = jnp.float32
BF16 = jnp.bfloat16
VMEM_LIMIT = 44 * 1024 * 1024


def tile_of(size, most):
    tile = min(size, most)
    while size % tile:
        tile -= 128
    return tile


def params():
    return pltpu.CompilerParams(vmem_limit_bytes=VMEM_LIMIT)


def gate_up_kernel(slot, parts, info, own, *refs):
    pieces = refs[:3 * parts]
    gate_ref, up_ref, out_ref, held, gate_held, up_held, gate_sems, up_sems = refs[3 * parts:]
    chunks, deep, depth, columns = gate_held.shape
    part = held.shape[1] // parts
    block, expert, wid, hid = info[slot, 0], info[slot, 1], info[8, 0], info[8, 1]
    away = jnp.bitwise_xor(block, wid)
    core = jnp.bitwise_and(hid, 1)

    def copies(n, i):
        rows = pl.ds(i * depth, depth)
        there = pl.ds(pl.multiple_of(n * columns, 128), columns)
        return (
            pltpu.make_async_copy(gate_ref.at[expert, rows, there], gate_held.at[n, i], gate_sems.at[n, i]),
            pltpu.make_async_copy(up_ref.at[expert, rows, there], up_held.at[n, i], up_sems.at[n, i]),
        )

    for i in range(deep):
        for copy in copies(0, i):
            copy.start()

    @pl.when(away == 0)
    def _():
        held[...] = own[...]

    for r, odd in ((1, 0), (1, 1), (2, 0), (2, 1), (3, None)):
        @pl.when((away == r) if odd is None else (away == r) & (core == odd))
        def _(r=r, odd=odd):
            for j in range(parts):
                step = 2 if odd is None else int(r != 1 + ((odd + j) % 2))
                q = jnp.bitwise_xor(hid, j)
                held[:, pl.ds(pl.multiple_of(q * part, 128), part)] = pieces[step * parts + j][...]

    @pl.loop(0, chunks)
    def _(n):
        gate = up = None
        for i in range(deep):
            for copy in copies(n, i):
                copy.wait()

            @pl.when(n + 1 < chunks)
            def _(i=i):
                for copy in copies(n + 1, i):
                    copy.start()

            rows = held[:, i * depth:(i + 1) * depth]
            more_gate = jnp.dot(rows, gate_held[n, i], preferred_element_type=F32)
            more_up = jnp.dot(rows, up_held[n, i], preferred_element_type=F32)
            gate = more_gate if gate is None else gate + more_gate
            up = more_up if up is None else up + more_up
        there = pl.ds(pl.multiple_of(n * columns, 128), columns)
        out_ref[:, there] = (gate / (1.0 + jnp.exp(-gate)) * up).astype(out_ref.dtype)


def gate_up(slot, info, own, pieces, gate_weight, up_weight):
    _, width, units = gate_weight.shape
    rows = own.shape[0]
    parts = len(pieces) // 3
    columns = tile_of(units, 256)
    deep = 4
    held = pltpu.VMEM((units // columns, deep, width // deep, columns), BF16)
    arrived = pltpu.SemaphoreType.DMA((units // columns, deep))
    anywhere = pl.BlockSpec(memory_space=pl.ANY)
    near = pl.BlockSpec(memory_space=pltpu.VMEM)
    return pl.pallas_call(
        functools.partial(gate_up_kernel, slot, parts),
        in_specs=[pl.BlockSpec(memory_space=pltpu.SMEM)] + [near] * (1 + len(pieces)) + [anywhere] * 2,
        out_specs=near,
        scratch_shapes=[pltpu.VMEM((rows, width), BF16), held, held, arrived, arrived],
        out_shape=jax.ShapeDtypeStruct((rows, units), BF16),
        compiler_params=params(),
        cost_estimate=pl.CostEstimate(
            flops=4 * rows * width * units,
            bytes_accessed=4 * width * units,
            transcendentals=rows * units,
        ),
        name="gate_up",
    )(info, own, *pieces, gate_weight, up_weight)


def down_kernel(slot, info, own, near, far, middle, end, weight_ref, coef_ref, out_ref, last, weight_held, weight_sems):
    expert, pair, wid = info[slot, 1], info[slot, 2], info[8, 0]
    inner = (wid == 1) | (wid == 2)
    chunks, deep, units, columns = weight_held.shape

    def weight_copy(n, r):
        rows = pl.ds(pl.multiple_of(jnp.bitwise_xor(wid, r) * units, units), units)
        there = pl.ds(pl.multiple_of(n * columns, 128), columns)
        return pltpu.make_async_copy(
            weight_ref.at[expert, rows, there], weight_held.at[n, r], weight_sems.at[n, r]
        )

    ahead = min(2, chunks)
    for n in range(ahead):
        for r in range(deep):
            weight_copy(n, r).start()

    @pl.when(inner)
    def _():
        last[...] = middle[...]

    @pl.when(jnp.logical_not(inner))
    def _():
        last[...] = end[...]

    @pl.loop(0, chunks)
    def _(n):
        part = None
        for r, ref in enumerate((own, near, far, last)):
            weight_copy(n, r).wait()

            @pl.when(n + ahead < chunks)
            def _(r=r):
                weight_copy(n + ahead, r).start()

            more = jnp.dot(ref[...], weight_held[n, r], preferred_element_type=F32)
            part = more if part is None else part + more
        there = pl.ds(pl.multiple_of(n * columns, 128), columns)
        out_ref[:, there] = coef_ref[pair] * part


def down(slot, info, shards, coef, down_weight):
    rows, units = shards[0].shape
    width = down_weight.shape[2]
    columns = tile_of(width, 256)
    near = pl.BlockSpec(memory_space=pltpu.VMEM)
    return pl.pallas_call(
        functools.partial(down_kernel, slot),
        in_specs=[pl.BlockSpec(memory_space=pltpu.SMEM)] + [near] * 5 + [pl.BlockSpec(memory_space=pl.ANY), near],
        out_specs=near,
        scratch_shapes=[
            pltpu.VMEM((rows, units), BF16),
            pltpu.VMEM((width // columns, 4, units, columns), BF16),
            pltpu.SemaphoreType.DMA((width // columns, 4)),
        ],
        out_shape=jax.ShapeDtypeStruct((rows, width), F32),
        compiler_params=params(),
        cost_estimate=pl.CostEstimate(
            flops=8 * rows * units * width, bytes_accessed=8 * units * width, transcendentals=0
        ),
        name="down",
    )(info, *shards, down_weight, coef)


FAR = [(0, 2), (2, 0), (1, 3), (3, 1)]
NEAR = [(0, 1), (1, 0), (2, 3), (3, 2)]
MIDDLE = [(1, 2), (2, 1)]
OUTWARD = [(1, 0), (2, 3)]
ACROSS = [(0, 2), (2, 0), (1, 3), (3, 1)]
TWIN = [(0, 1), (1, 0), (2, 3), (3, 2)]


def both(even, odd):
    return [(w * 4 + h, (w ^ (odd if h % 2 else even)) * 4 + h) for w in range(4) for h in range(4)]


FIRST = both(1, 2)
SECOND = both(2, 1)


def after(value, *done):
    return lax.optimization_barrier((value, *done))[0]


def sparse_device(tokens, gate_weight, up_weight, down_weight, routes, combine):
    experts = gate_weight.shape[0]
    blocks = routes.shape[0]
    rows = combine.shape[0] // blocks
    wid = lax.axis_index("wid")
    hid = lax.axis_index("hid")
    inner = (wid == 1) | (wid == 2)

    labels = jnp.arange(experts, dtype=jnp.int32)
    picked = routes[:, :, None] == labels[None, None, :]
    coef = jnp.sum(combine.reshape(blocks, rows, -1)[:, :, :, None] * picked.astype(F32)[:, None], axis=2)
    coef = jnp.transpose(coef, (0, 2, 1)).reshape(blocks * experts, rows, 1)
    named = jnp.any(picked, axis=1)
    flat = named.reshape(-1).astype(jnp.int32)
    place = jnp.cumsum(flat) - 1
    count = jnp.sum(flat)
    number = jnp.arange(blocks * experts, dtype=jnp.int32)
    hit = (place[None, :] == number[:, None]) & (flat[None, :] == 1)
    pair = jnp.sum(jnp.where(hit, number[None, :], 0), axis=1)
    block_of = pair // experts
    info = jnp.stack([block_of, pair % experts, pair], axis=1)
    here = jnp.stack([wid, hid, wid]).astype(jnp.int32)[None]
    info = jnp.concatenate([info, here], axis=0)

    core, x = hid % 2, hid // 2
    quarter = tokens.shape[1] // 4
    mine = lax.dynamic_slice_in_dim(tokens, hid * quarter, quarter, axis=1)
    first = lax.ppermute(mine, ("wid", "hid"), FIRST)
    first_across = lax.ppermute(first, "hid", ACROSS)
    second = lax.ppermute(after(mine, first), ("wid", "hid"), SECOND)
    second_across = lax.ppermute(second, "hid", ACROSS)
    middle = lax.ppermute(after(mine, second, first_across), "wid", MIDDLE)
    outer = lax.ppermute(after(jnp.where(core == 0, second, first), first_across), "wid", OUTWARD)
    last = jnp.where(inner, middle, outer)
    last_across = lax.ppermute(after(last, second_across), "hid", ACROSS)
    pieces = []
    for piece, across in ((first, first_across), (second, second_across), (last, last_across)):
        pieces += [piece, lax.ppermute(piece, "hid", TWIN), across, lax.ppermute(across, "hid", TWIN)]

    def outward(hidden, near, far):
        middle = lax.ppermute(after(hidden, far), "wid", MIDDLE)
        outer = lax.ppermute(far, "wid", OUTWARD)
        return hidden, near, far, middle, outer

    def inward(hidden):
        return hidden, lax.ppermute(hidden, "wid", NEAR), lax.ppermute(hidden, "wid", FAR)

    def share(parts, blocks, parity):
        sums = [
            sum(jnp.where(block == 2 * half + parity, part, 0.0) for part, block in zip(parts, blocks))
            for half in range(2)
        ]
        return jnp.stack(sums)

    most = 4

    def branch(slots, more):
        def run(info, coef, *pieces):
            first, second, parts = [], [], []
            for slot in range(slots + 1):
                if slot < slots:
                    ready = info if slot < 2 else after(info, first[slot - 2][2])
                    first.append(inward(gate_up(slot, ready, tokens, pieces, gate_weight, up_weight)))
                if slot >= 2:
                    ready = info if slot >= slots else after(info, first[slot][0])
                    parts.append(down(slot - 2, ready, second[slot - 2], coef, down_weight))
                if slot >= 1:
                    hidden, near, far = first[slot - 1]
                    far = far if slot < 2 else after(far, parts[-1])
                    second.append(outward(hidden, near, far))
            parts.append(down(slots - 1, info, second[slots - 1], coef, down_weight))
            kept = share(parts, block_of, core)
            to_twin = share(parts, block_of, 1 - core)
            if more:

                def further(state):
                    at, kept, to_twin = state
                    one = jnp.concatenate([lax.dynamic_slice_in_dim(info, at, 1, axis=0), info[1:]], axis=0)
                    sent = outward(*inward(gate_up(0, one, tokens, pieces, gate_weight, up_weight)))
                    part, block = [down(0, one, sent, coef, down_weight)], [one[0, 0]]
                    return at + 1, kept + share(part, block, core), to_twin + share(part, block, 1 - core)

                state = (jnp.int32(slots), kept, to_twin)
                _, kept, to_twin = lax.while_loop(lambda state: state[0] < count, further, state)
            return kept, to_twin.astype(BF16)

        return run

    branches = [branch(n + 1, False) for n in range(most)] + [branch(most, True)]
    kept, to_twin = lax.switch(jnp.minimum(count, most + 1) - 1, branches, info, coef, *pieces)

    kept = kept + lax.ppermute(to_twin, "hid", TWIN).astype(F32)
    to_across = lax.dynamic_index_in_dim(kept, 1 - x, axis=0, keepdims=False).astype(BF16)
    own = lax.dynamic_index_in_dim(kept, x, axis=0, keepdims=False)
    return (own + lax.ppermute(to_across, "hid", ACROSS).astype(F32)).astype(BF16)


def dense_device(tokens, gate_weight, up_weight, down_weight, routes, combine):
    experts = gate_weight.shape[0]
    block = combine.shape[0] // routes.shape[0]
    rows_route = jnp.repeat(routes, block, axis=0)
    labels = jnp.arange(experts, dtype=jnp.int32)
    picked = (rows_route[:, :, None] == labels[None, None, :]).astype(F32)
    weights = jnp.sum(combine[:, :, None] * picked, axis=1)
    piece = lax.all_gather(tokens, "wid", axis=0, tiled=True)
    gate = jnp.einsum("td,edf->etf", piece, gate_weight, preferred_element_type=F32)
    upward = jnp.einsum("td,edf->etf", piece, up_weight, preferred_element_type=F32)
    hidden = (jax.nn.silu(gate) * upward).astype(BF16)
    summed = jnp.einsum(
        "etf,efd->etd",
        lax.all_gather(hidden, "wid", axis=2, tiled=True),
        down_weight,
        preferred_element_type=F32,
    )
    partial_value = jnp.sum(jnp.transpose(weights)[:, :, None] * summed, axis=0)
    own_rows = lax.psum_scatter(partial_value, "hid", scatter_dimension=0, tiled=True)
    return own_rows.astype(BF16)


def solution(mesh):
    placed = (
        P(("grp", "wid"), None),
        P(None, None, ("hid", "wid")),
        P(None, None, ("hid", "wid")),
        P(None, "hid", "wid"),
        P("grp", None),
        P("grp", None),
    )

    def program(tokens, gate_weight, up_weight, down_weight, routes, combine):
        blocks = routes.shape[0] // mesh.shape["grp"]
        square = mesh.shape["wid"] == 4 and mesh.shape["hid"] == 4 and blocks == 4
        return jax.shard_map(
            sparse_device if square else dense_device,
            mesh=mesh,
            in_specs=placed,
            out_specs=P(("grp", "hid"), "wid"),
            check_vma=False,
        )(tokens, gate_weight, up_weight, down_weight, routes, combine)

    return program
```

```python
import functools

import jax
import jax.numpy as jnp
from jax import lax
from jax.experimental import pallas as pl
from jax.experimental.pallas import tpu as pltpu
from jax.sharding import PartitionSpec as P

F32 = jnp.float32
BF16 = jnp.bfloat16
VMEM_LIMIT = 40 * 1024 * 1024


def tile_of(size, most):
    tile = min(size, most)
    while size % tile:
        tile -= 128
    return tile


def params():
    return pltpu.CompilerParams(vmem_limit_bytes=VMEM_LIMIT)


SHORT = pl.CostEstimate(flops=1000, bytes_accessed=1000, transcendentals=0)


def gate_up_kernel(slot, parts, info, *refs):
    pieces = refs[:4 * parts]
    gate_ref, up_ref, out_ref, held, gate_held, up_held, gate_sum, up_sum, sems, gate_sems, up_sems = refs[4 * parts:]
    chunks, _, depth, columns = gate_held.shape
    block, expert, wid, hid = info[slot, 0], info[slot, 1], info[8, 0], info[8, 1]
    away = jnp.bitwise_xor(block, wid)

    for r in range(4):
        @pl.when(away == r)
        def _(r=r):
            for j in range(parts):
                q = jnp.bitwise_xor(hid, j) if r else j
                pltpu.make_async_copy(pieces[r * parts + j], held.at[q], sems.at[q]).start()

    def copies(n, q):
        rows = pl.ds(pl.multiple_of(q * depth, depth), depth)
        there = pl.ds(pl.multiple_of(n * columns, 128), columns)
        return (
            pltpu.make_async_copy(gate_ref.at[expert, rows, there], gate_held.at[n, q], gate_sems.at[n, q]),
            pltpu.make_async_copy(up_ref.at[expert, rows, there], up_held.at[n, q], up_sems.at[n, q]),
        )

    @pl.loop(0, parts)
    def _(q):
        for copy in copies(0, q):
            copy.start()

    @pl.loop(0, parts)
    def _(q):
        pltpu.make_async_copy(pieces[0], held.at[q], sems.at[q]).wait()

    @pl.loop(0, chunks)
    def _(n):
        gate_sum[...] = jnp.zeros_like(gate_sum)
        up_sum[...] = jnp.zeros_like(up_sum)

        @pl.loop(0, parts)
        def _(q):
            @pl.when(n + 1 < chunks)
            def _():
                for copy in copies(n + 1, q):
                    copy.start()

            for copy in copies(n, q):
                copy.wait()
            gate_sum[...] += jnp.dot(held[q], gate_held[n, q], preferred_element_type=F32)
            up_sum[...] += jnp.dot(held[q], up_held[n, q], preferred_element_type=F32)

        gate = gate_sum[...]
        there = pl.ds(pl.multiple_of(n * columns, 128), columns)
        out_ref[:, there] = (gate / (1.0 + jnp.exp(-gate)) * up_sum[...]).astype(out_ref.dtype)


def gate_up(slot, info, pieces, gate_weight, up_weight):
    _, width, units = gate_weight.shape
    rows = pieces[0].shape[0]
    parts = len(pieces) // 4
    columns = tile_of(units, 256)
    held = pltpu.VMEM((units // columns, parts, width // parts, columns), BF16)
    total = pltpu.VMEM((rows, columns), F32)
    arrived = pltpu.SemaphoreType.DMA((units // columns, parts))
    anywhere = pl.BlockSpec(memory_space=pl.ANY)
    return pl.pallas_call(
        functools.partial(gate_up_kernel, slot, parts),
        in_specs=[pl.BlockSpec(memory_space=pltpu.SMEM)] + [anywhere] * (2 + len(pieces)),
        out_specs=pl.BlockSpec(memory_space=pltpu.VMEM),
        scratch_shapes=[
            pltpu.VMEM((parts, rows, width // parts), BF16),
            held,
            held,
            total,
            total,
            pltpu.SemaphoreType.DMA((parts,)),
            arrived,
            arrived,
        ],
        out_shape=jax.ShapeDtypeStruct((rows, units), BF16),
        compiler_params=params(),
        cost_estimate=SHORT,
        name="gate_up",
    )(info, *pieces, gate_weight, up_weight)


def down_kernel(slot, info, own, near, far, middle, end, weight_ref, coef_ref, out_ref, last, weight_held, weight_sems):
    expert, pair, wid = info[slot, 1], info[slot, 2], info[8, 0]
    inner = (wid == 1) | (wid == 2)
    chunks, deep, units, columns = weight_held.shape

    def weight_copy(n, r):
        rows = pl.ds(pl.multiple_of(jnp.bitwise_xor(wid, r) * units, units), units)
        there = pl.ds(pl.multiple_of(n * columns, 128), columns)
        return pltpu.make_async_copy(
            weight_ref.at[expert, rows, there], weight_held.at[n, r], weight_sems.at[n, r]
        )

    ahead = min(2, chunks)

    @pl.loop(0, ahead)
    def _(n):
        for r in range(deep):
            weight_copy(n, r).start()

    @pl.when(inner)
    def _():
        last[...] = middle[...]

    @pl.when(jnp.logical_not(inner))
    def _():
        last[...] = end[...]

    @pl.loop(0, chunks)
    def _(n):
        part = None
        for r, ref in enumerate((own, near, far, last)):
            weight_copy(n, r).wait()

            @pl.when(n + ahead < chunks)
            def _(r=r):
                weight_copy(n + ahead, r).start()

            more = jnp.dot(ref[...], weight_held[n, r], preferred_element_type=F32)
            part = more if part is None else part + more
        there = pl.ds(pl.multiple_of(n * columns, 128), columns)
        out_ref[:, there] = coef_ref[pair] * part


def down(slot, info, shards, coef, down_weight):
    rows, units = shards[0].shape
    width = down_weight.shape[2]
    columns = tile_of(width, 256)
    near = pl.BlockSpec(memory_space=pltpu.VMEM)
    return pl.pallas_call(
        functools.partial(down_kernel, slot),
        in_specs=[pl.BlockSpec(memory_space=pltpu.SMEM)] + [near] * 5 + [pl.BlockSpec(memory_space=pl.ANY), near],
        out_specs=near,
        scratch_shapes=[
            pltpu.VMEM((rows, units), BF16),
            pltpu.VMEM((width // columns, 4, units, columns), BF16),
            pltpu.SemaphoreType.DMA((width // columns, 4)),
        ],
        out_shape=jax.ShapeDtypeStruct((rows, width), F32),
        compiler_params=params(),
        cost_estimate=SHORT,
        name="down",
    )(info, *shards, down_weight, coef)


FAR = [(0, 2), (2, 0), (1, 3), (3, 1)]
NEAR = [(0, 1), (1, 0), (2, 3), (3, 2)]
MIDDLE = [(1, 2), (2, 1)]
OUTWARD = [(1, 0), (2, 3)]
ACROSS = [(0, 2), (2, 0), (1, 3), (3, 1)]
TWIN = [(0, 1), (1, 0), (2, 3), (3, 2)]


def after(value, *done):
    return lax.optimization_barrier((value, *done))[0]


def sparse_device(tokens, gate_weight, up_weight, down_weight, routes, combine):
    experts = gate_weight.shape[0]
    blocks = routes.shape[0]
    rows = combine.shape[0] // blocks
    wid = lax.axis_index("wid")
    hid = lax.axis_index("hid")
    inner = (wid == 1) | (wid == 2)

    labels = jnp.arange(experts, dtype=jnp.int32)
    picked = routes[:, :, None] == labels[None, None, :]
    coef = jnp.sum(combine.reshape(blocks, rows, -1)[:, :, :, None] * picked.astype(F32)[:, None], axis=2)
    coef = jnp.transpose(coef, (0, 2, 1)).reshape(blocks * experts, rows, 1)
    named = jnp.any(picked, axis=1)
    flat = named.reshape(-1).astype(jnp.int32)
    place = jnp.cumsum(flat) - 1
    count = jnp.sum(flat)
    number = jnp.arange(blocks * experts, dtype=jnp.int32)
    hit = (place[None, :] == number[:, None]) & (flat[None, :] == 1)
    pair = jnp.sum(jnp.where(hit, number[None, :], 0), axis=1)
    block_of = pair // experts
    info = jnp.stack([block_of, pair % experts, pair], axis=1)
    here = jnp.stack([wid, hid, wid]).astype(jnp.int32)[None]
    info = jnp.concatenate([info, here], axis=0)

    core, x = hid % 2, hid // 2
    quarter = tokens.shape[1] // 4
    mine = lax.dynamic_slice_in_dim(tokens, hid * quarter, quarter, axis=1)
    near = lax.ppermute(mine, "wid", NEAR)
    far = lax.ppermute(mine, "wid", FAR)
    middle = lax.ppermute(mine, "wid", MIDDLE)
    near_across = lax.ppermute(near, "hid", ACROSS)
    outer = lax.ppermute(after(far, near), "wid", OUTWARD)
    far_across = lax.ppermute(far, "hid", ACROSS)
    last = jnp.where(inner, middle, outer)
    last_across = lax.ppermute(last, "hid", ACROSS)
    pieces = [tokens[:, q * quarter:(q + 1) * quarter] for q in range(4)]
    for piece, across in ((near, near_across), (far, far_across), (last, last_across)):
        pieces += [piece, lax.ppermute(piece, "hid", TWIN), across, lax.ppermute(across, "hid", TWIN)]

    def outward(hidden, near, far):
        middle = lax.ppermute(after(hidden, far), "wid", MIDDLE)
        outer = lax.ppermute(far, "wid", OUTWARD)
        return hidden, near, far, middle, outer

    def inward(hidden):
        return hidden, lax.ppermute(hidden, "wid", NEAR), lax.ppermute(hidden, "wid", FAR)

    def shares(parts, blocks):
        at = [2 * (1 - x) + 1 - core, 2 * (1 - x) + core, 2 * x + 1 - core, 2 * x + core]
        return [sum(jnp.where(block == b, part, 0.0) for part, block in zip(parts, blocks)) for b in at]

    def reduced(diagonal, across, twin, own):
        across = across + lax.ppermute(diagonal.astype(BF16), "hid", TWIN).astype(F32)
        own = own + lax.ppermute(twin.astype(BF16), "hid", TWIN).astype(F32)
        return (own + lax.ppermute(across.astype(BF16), "hid", ACROSS).astype(F32)).astype(BF16)

    most = 4

    def branch(slots, more):
        def run(info, coef, *pieces):
            first, second, parts = [], [], []
            for slot in range(slots + 1):
                if slot < slots:
                    ready = info if slot < 2 else after(info, first[slot - 2][2])
                    first.append(inward(gate_up(slot, ready, pieces, gate_weight, up_weight)))
                if slot >= 1:
                    second.append(outward(*first[slot - 1]))
                if slot >= 2:
                    ready = after(info, first[slot - 1][2]) if slot == slots else after(info, first[slot - 1][2], first[slot][0])
                    parts.append(down(slot - 2, ready, second[slot - 2], coef, down_weight))
            parts.append(down(slots - 1, info, second[slots - 1], coef, down_weight))
            sums = shares(parts, [info[slot, 0] for slot in range(slots)])
            if more:

                def further(state):
                    at, *sums = state
                    one = jnp.concatenate([lax.dynamic_slice_in_dim(info, at, 1, axis=0), info[1:]], axis=0)
                    sent = outward(*inward(gate_up(0, one, pieces, gate_weight, up_weight)))
                    part = down(0, one, sent, coef, down_weight)
                    return at + 1, *[old + new for old, new in zip(sums, shares([part], [one[0, 0]]))]

                _, *sums = lax.while_loop(lambda state: state[0] < count, further, (jnp.int32(slots), *sums))
            return reduced(*sums)

        return run

    branches = [branch(n + 1, False) for n in range(most)] + [branch(most, True)]
    return lax.switch(jnp.minimum(count, most + 1) - 1, branches, info, coef, *pieces)


def dense_device(tokens, gate_weight, up_weight, down_weight, routes, combine):
    experts = gate_weight.shape[0]
    block = combine.shape[0] // routes.shape[0]
    rows_route = jnp.repeat(routes, block, axis=0)
    labels = jnp.arange(experts, dtype=jnp.int32)
    picked = (rows_route[:, :, None] == labels[None, None, :]).astype(F32)
    weights = jnp.sum(combine[:, :, None] * picked, axis=1)
    piece = lax.all_gather(tokens, "wid", axis=0, tiled=True)
    gate = jnp.einsum("td,edf->etf", piece, gate_weight, preferred_element_type=F32)
    upward = jnp.einsum("td,edf->etf", piece, up_weight, preferred_element_type=F32)
    hidden = (jax.nn.silu(gate) * upward).astype(BF16)
    summed = jnp.einsum(
        "etf,efd->etd",
        lax.all_gather(hidden, "wid", axis=2, tiled=True),
        down_weight,
        preferred_element_type=F32,
    )
    partial_value = jnp.sum(jnp.transpose(weights)[:, :, None] * summed, axis=0)
    own_rows = lax.psum_scatter(partial_value, "hid", scatter_dimension=0, tiled=True)
    return own_rows.astype(BF16)


def solution(mesh):
    placed = (
        P(("grp", "wid"), None),
        P(None, None, ("hid", "wid")),
        P(None, None, ("hid", "wid")),
        P(None, "hid", "wid"),
        P("grp", None),
        P("grp", None),
    )

    def program(tokens, gate_weight, up_weight, down_weight, routes, combine):
        blocks = routes.shape[0] // mesh.shape["grp"]
        square = mesh.shape["wid"] == 4 and mesh.shape["hid"] == 4 and blocks == 4
        return jax.shard_map(
            sparse_device if square else dense_device,
            mesh=mesh,
            in_specs=placed,
            out_specs=P(("grp", "hid"), "wid"),
            check_vma=False,
        )(tokens, gate_weight, up_weight, down_weight, routes, combine)

    return program
```

```python
import functools

import jax
import jax.numpy as jnp
from jax import lax
from jax.experimental import pallas as pl
from jax.experimental.pallas import tpu as pltpu
from jax.sharding import PartitionSpec as P

F32 = jnp.float32
BF16 = jnp.bfloat16
VMEM_LIMIT = 40 * 1024 * 1024


def tile_of(size, most):
    tile = min(size, most)
    while size % tile:
        tile -= 128
    return tile


def params():
    return pltpu.CompilerParams(vmem_limit_bytes=VMEM_LIMIT)


def named_kernel(experts, routes, info, number):
    blocks, choices = routes.shape
    slots = blocks * experts
    for slot in range(slots):
        info[slot, 0] = 0
        info[slot, 1] = 0
    info[slots, 0] = lax.axis_index("wid")
    info[slots, 1] = lax.axis_index("hid")
    count = jnp.int32(0)
    for block in range(blocks):
        for expert in range(experts):
            named = routes[block, 0] == expert
            for choice in range(1, choices):
                named = named | (routes[block, choice] == expert)

            @pl.when(named)
            def _(block=block, expert=expert, count=count):
                info[count, 0] = block
                info[count, 1] = expert

            count = count + named.astype(jnp.int32)
    number[0] = count


def named_pairs(experts, routes):
    scalars = pl.BlockSpec(memory_space=pltpu.SMEM)
    return pl.pallas_call(
        functools.partial(named_kernel, experts),
        in_specs=[scalars],
        out_specs=[scalars, scalars],
        out_shape=[
            jax.ShapeDtypeStruct((routes.shape[0] * experts + 1, 2), jnp.int32),
            jax.ShapeDtypeStruct((1,), jnp.int32),
        ],
        name="named",
    )(routes)


SHORT = pl.CostEstimate(flops=1000, bytes_accessed=1000, transcendentals=0)


def gate_up_kernel(slot, parts, info, *refs):
    pieces = refs[:4 * parts]
    gate_ref, up_ref, out_ref, held, gate_held, up_held, gate_sum, up_sum, sems, gate_sems, up_sems = refs[4 * parts:]
    chunks, _, depth, columns = gate_held.shape
    block, expert, wid, hid = info[slot, 0], info[slot, 1], info[8, 0], info[8, 1]
    away = jnp.bitwise_xor(block, wid)

    for r in range(4):
        @pl.when(away == r)
        def _(r=r):
            for j in range(parts):
                q = jnp.bitwise_xor(hid, j) if r else j
                pltpu.make_async_copy(pieces[r * parts + j], held.at[q], sems.at[q]).start()

    def copies(n, q):
        rows = pl.ds(pl.multiple_of(q * depth, depth), depth)
        there = pl.ds(pl.multiple_of(n * columns, 128), columns)
        return (
            pltpu.make_async_copy(gate_ref.at[expert, rows, there], gate_held.at[n, q], gate_sems.at[n, q]),
            pltpu.make_async_copy(up_ref.at[expert, rows, there], up_held.at[n, q], up_sems.at[n, q]),
        )

    @pl.loop(0, parts)
    def _(q):
        for copy in copies(0, q):
            copy.start()

    @pl.loop(0, parts)
    def _(q):
        pltpu.make_async_copy(pieces[0], held.at[q], sems.at[q]).wait()

    @pl.loop(0, chunks)
    def _(n):
        gate_sum[...] = jnp.zeros_like(gate_sum)
        up_sum[...] = jnp.zeros_like(up_sum)

        @pl.loop(0, parts)
        def _(q):
            @pl.when(n + 1 < chunks)
            def _():
                for copy in copies(n + 1, q):
                    copy.start()

            for copy in copies(n, q):
                copy.wait()
            gate_sum[...] += jnp.dot(held[q], gate_held[n, q], preferred_element_type=F32)
            up_sum[...] += jnp.dot(held[q], up_held[n, q], preferred_element_type=F32)

        gate = gate_sum[...]
        there = pl.ds(pl.multiple_of(n * columns, 128), columns)
        out_ref[:, there] = (gate / (1.0 + jnp.exp(-gate)) * up_sum[...]).astype(out_ref.dtype)


def gate_up(slot, info, pieces, gate_weight, up_weight):
    _, width, units = gate_weight.shape
    rows = pieces[0].shape[0]
    parts = len(pieces) // 4
    columns = tile_of(units, 256)
    held = pltpu.VMEM((units // columns, parts, width // parts, columns), BF16)
    total = pltpu.VMEM((rows, columns), F32)
    arrived = pltpu.SemaphoreType.DMA((units // columns, parts))
    anywhere = pl.BlockSpec(memory_space=pl.ANY)
    return pl.pallas_call(
        functools.partial(gate_up_kernel, slot, parts),
        in_specs=[pl.BlockSpec(memory_space=pltpu.SMEM)] + [anywhere] * (2 + len(pieces)),
        out_specs=pl.BlockSpec(memory_space=pltpu.VMEM),
        scratch_shapes=[
            pltpu.VMEM((parts, rows, width // parts), BF16),
            held,
            held,
            total,
            total,
            pltpu.SemaphoreType.DMA((parts,)),
            arrived,
            arrived,
        ],
        out_shape=jax.ShapeDtypeStruct((rows, units), BF16),
        compiler_params=params(),
        cost_estimate=pl.CostEstimate(
            flops=4 * rows * width * units,
            bytes_accessed=4 * width * units,
            transcendentals=rows * units,
        ),
        name="gate_up",
    )(info, *pieces, gate_weight, up_weight)


def down_kernel(slot, info, own, near, far, middle, end, weight_ref, combine_ref, routes, out_ref, last, weight_held, weight_sems):
    block, expert, wid = info[slot, 0], info[slot, 1], info[8, 0]
    inner = (wid == 1) | (wid == 2)
    chunks, deep, units, columns = weight_held.shape

    def weight_copy(n, r):
        rows = pl.ds(pl.multiple_of(jnp.bitwise_xor(wid, r) * units, units), units)
        there = pl.ds(pl.multiple_of(n * columns, 128), columns)
        return pltpu.make_async_copy(
            weight_ref.at[expert, rows, there], weight_held.at[n, r], weight_sems.at[n, r]
        )

    ahead = min(2, chunks)

    @pl.loop(0, ahead)
    def _(n):
        for r in range(deep):
            weight_copy(n, r).start()

    @pl.when(inner)
    def _():
        last[...] = middle[...]

    @pl.when(jnp.logical_not(inner))
    def _():
        last[...] = end[...]

    choices = combine_ref.shape[2]
    coef = sum(jnp.where(routes[block, c] == expert, combine_ref[block, :, c:c + 1], 0.0) for c in range(choices))

    @pl.loop(0, chunks)
    def _(n):
        part = None
        for r, ref in enumerate((own, near, far, last)):
            weight_copy(n, r).wait()

            @pl.when(n + ahead < chunks)
            def _(r=r):
                weight_copy(n + ahead, r).start()

            more = jnp.dot(ref[...], weight_held[n, r], preferred_element_type=F32)
            part = more if part is None else part + more
        there = pl.ds(pl.multiple_of(n * columns, 128), columns)
        out_ref[:, there] = coef * part


def down(slot, info, shards, combine, routes, down_weight):
    rows, units = shards[0].shape
    width = down_weight.shape[2]
    columns = tile_of(width, 256)
    near = pl.BlockSpec(memory_space=pltpu.VMEM)
    return pl.pallas_call(
        functools.partial(down_kernel, slot),
        in_specs=[pl.BlockSpec(memory_space=pltpu.SMEM)] + [near] * 5 + [pl.BlockSpec(memory_space=pl.ANY), near, pl.BlockSpec(memory_space=pltpu.SMEM)],
        out_specs=near,
        scratch_shapes=[
            pltpu.VMEM((rows, units), BF16),
            pltpu.VMEM((width // columns, 4, units, columns), BF16),
            pltpu.SemaphoreType.DMA((width // columns, 4)),
        ],
        out_shape=jax.ShapeDtypeStruct((rows, width), F32),
        compiler_params=params(),
        cost_estimate=SHORT,
        name="down",
    )(info, *shards, down_weight, combine, routes)


FAR = [(0, 2), (2, 0), (1, 3), (3, 1)]
NEAR = [(0, 1), (1, 0), (2, 3), (3, 2)]
MIDDLE = [(1, 2), (2, 1)]
OUTWARD = [(1, 0), (2, 3)]
ACROSS = [(0, 2), (2, 0), (1, 3), (3, 1)]
TWIN = [(0, 1), (1, 0), (2, 3), (3, 2)]


def spread(tokens, wid, hid):
    quarter = tokens.shape[1] // 4
    mine = lax.dynamic_slice_in_dim(tokens, hid * quarter, quarter, axis=1)
    far = lax.ppermute(mine, "wid", FAR)
    near = lax.ppermute(mine, "wid", NEAR)
    near_across = lax.ppermute(near, "hid", ACROSS)
    middle = lax.ppermute(after(mine, near), "wid", MIDDLE)
    outer = lax.ppermute(far, "wid", OUTWARD)
    far_across = lax.ppermute(far, "hid", ACROSS)
    third = jnp.where((wid == 1) | (wid == 2), middle, outer)
    third_across = lax.ppermute(third, "hid", ACROSS)
    pieces = [tokens[:, q * quarter:(q + 1) * quarter] for q in range(4)]
    for piece, across in ((near, near_across), (far, far_across), (third, third_across)):
        pieces += [piece, lax.ppermute(piece, "hid", TWIN), across, lax.ppermute(across, "hid", TWIN)]
    return pieces


def after(value, *done):
    return lax.optimization_barrier((value, *done))[0]


def sparse_device(tokens, gate_weight, up_weight, down_weight, routes, combine):
    experts = gate_weight.shape[0]
    blocks = routes.shape[0]
    rows = combine.shape[0] // blocks
    wid = lax.axis_index("wid")
    hid = lax.axis_index("hid")
    core, x = hid % 2, hid // 2
    info, number = named_pairs(experts, routes)
    count = number[0]
    combine = combine.reshape(blocks, rows, -1)
    pieces = spread(tokens, wid, hid)

    def outward(hidden, near, far):
        middle = lax.ppermute(after(hidden, far), "wid", MIDDLE)
        outer = lax.ppermute(far, "wid", OUTWARD)
        return hidden, near, far, middle, outer

    def inward(hidden):
        return hidden, lax.ppermute(hidden, "wid", NEAR), lax.ppermute(hidden, "wid", FAR)

    def shares(parts, blocks):
        at = [2 * (1 - x) + 1 - core, 2 * (1 - x) + core, 2 * x + 1 - core, 2 * x + core]
        return [sum(jnp.where(block == b, part, 0.0) for part, block in zip(parts, blocks)) for b in at]

    def reduced(diagonal, across, twin, own):
        across = across + lax.ppermute(diagonal.astype(BF16), "hid", TWIN).astype(F32)
        own = own + lax.ppermute(twin.astype(BF16), "hid", TWIN).astype(F32)
        arriving = lax.ppermute(across.astype(BF16), "hid", ACROSS)
        return (lax.optimization_barrier(own) + arriving.astype(F32)).astype(BF16)

    most = 4

    def branch(slots, more):
        def run(info, combine, routes, *pieces):
            first, second, parts = [], [], []
            for slot in range(slots + 1):
                if slot < slots:
                    ready = info if slot < 2 else after(info, *first[slot - 2][1:])
                    first.append(inward(gate_up(slot, ready, pieces, gate_weight, up_weight)))
                if slot >= 1:
                    hidden, near, far = first[slot - 1]
                    second.append(outward(hidden, near, after(far, parts[-1]) if parts else far))
                if slot >= 2:
                    ready = after(info, *first[slot - 1][1:], *(first[slot][:1] if slot < slots else ()))
                    parts.append(down(slot - 2, ready, second[slot - 2], combine, routes, down_weight))
            parts.append(down(slots - 1, info, second[slots - 1], combine, routes, down_weight))
            sums = shares(parts, [info[slot, 0] for slot in range(slots)])
            if more:

                def further(state):
                    at, *sums = state
                    one = jnp.concatenate([lax.dynamic_slice_in_dim(info, at, 1, axis=0), info[1:]], axis=0)
                    sent = outward(*inward(gate_up(0, one, pieces, gate_weight, up_weight)))
                    part = down(0, one, sent, combine, routes, down_weight)
                    return at + 1, *[old + new for old, new in zip(sums, shares([part], [one[0, 0]]))]

                _, *sums = lax.while_loop(lambda state: state[0] < count, further, (jnp.int32(slots), *sums))
            return reduced(*sums)

        return run

    branches = [branch(n + 1, False) for n in range(most)] + [branch(most, True)]
    return lax.switch(jnp.minimum(count, most + 1) - 1, branches, info, combine, routes, *pieces)


def dense_device(tokens, gate_weight, up_weight, down_weight, routes, combine):
    experts = gate_weight.shape[0]
    block = combine.shape[0] // routes.shape[0]
    rows_route = jnp.repeat(routes, block, axis=0)
    labels = jnp.arange(experts, dtype=jnp.int32)
    picked = (rows_route[:, :, None] == labels[None, None, :]).astype(F32)
    weights = jnp.sum(combine[:, :, None] * picked, axis=1)
    piece = lax.all_gather(tokens, "wid", axis=0, tiled=True)
    gate = jnp.einsum("td,edf->etf", piece, gate_weight, preferred_element_type=F32)
    upward = jnp.einsum("td,edf->etf", piece, up_weight, preferred_element_type=F32)
    hidden = (jax.nn.silu(gate) * upward).astype(BF16)
    summed = jnp.einsum(
        "etf,efd->etd",
        lax.all_gather(hidden, "wid", axis=2, tiled=True),
        down_weight,
        preferred_element_type=F32,
    )
    partial_value = jnp.sum(jnp.transpose(weights)[:, :, None] * summed, axis=0)
    own_rows = lax.psum_scatter(partial_value, "hid", scatter_dimension=0, tiled=True)
    return own_rows.astype(BF16)


def solution(mesh):
    placed = (
        P(("grp", "wid"), None),
        P(None, None, ("hid", "wid")),
        P(None, None, ("hid", "wid")),
        P(None, "hid", "wid"),
        P("grp", None),
        P("grp", None),
    )

    def program(tokens, gate_weight, up_weight, down_weight, routes, combine):
        blocks = routes.shape[0] // mesh.shape["grp"]
        square = mesh.shape["wid"] == 4 and mesh.shape["hid"] == 4 and blocks == 4
        return jax.shard_map(
            sparse_device if square else dense_device,
            mesh=mesh,
            in_specs=placed,
            out_specs=P(("grp", "hid"), "wid"),
            check_vma=False,
        )(tokens, gate_weight, up_weight, down_weight, routes, combine)

    return program
```

```python
import functools

import jax
import jax.numpy as jnp
from jax import lax
from jax.experimental import pallas as pl
from jax.experimental.pallas import tpu as pltpu
from jax.sharding import PartitionSpec as P

F32 = jnp.float32
BF16 = jnp.bfloat16
VMEM_LIMIT = 40 * 1024 * 1024


def tile_of(size, most):
    tile = min(size, most)
    while size % tile:
        tile -= 128
    return tile


def params():
    return pltpu.CompilerParams(vmem_limit_bytes=VMEM_LIMIT)


def named_kernel(experts, routes, info, number):
    blocks, choices = routes.shape
    slots = blocks * experts
    for slot in range(slots):
        info[slot, 0] = 0
        info[slot, 1] = 0
    info[slots, 0] = lax.axis_index("wid")
    info[slots, 1] = lax.axis_index("hid")
    count = jnp.int32(0)
    for block in range(blocks):
        for expert in range(experts):
            named = routes[block, 0] == expert
            for choice in range(1, choices):
                named = named | (routes[block, choice] == expert)

            @pl.when(named)
            def _(block=block, expert=expert, count=count):
                info[count, 0] = block
                info[count, 1] = expert

            count = count + named.astype(jnp.int32)
    number[0] = count


def named_pairs(experts, routes):
    scalars = pl.BlockSpec(memory_space=pltpu.SMEM)
    return pl.pallas_call(
        functools.partial(named_kernel, experts),
        in_specs=[scalars],
        out_specs=[scalars, scalars],
        out_shape=[
            jax.ShapeDtypeStruct((routes.shape[0] * experts + 1, 2), jnp.int32),
            jax.ShapeDtypeStruct((1,), jnp.int32),
        ],
        name="named",
    )(routes)


SHORT = pl.CostEstimate(flops=1000, bytes_accessed=1000, transcendentals=0)


def gate_up_kernel(slot, parts, info, *refs):
    pieces = refs[:4 * parts]
    gate_ref, up_ref, out_ref, held, gate_held, up_held, gate_sum, up_sum, sems, gate_sems, up_sems = refs[4 * parts:]
    chunks, _, depth, columns = gate_held.shape
    block, expert, wid, hid = info[slot, 0], info[slot, 1], info[8, 0], info[8, 1]
    away = jnp.bitwise_xor(block, wid)

    for r in range(4):
        @pl.when(away == r)
        def _(r=r):
            for j in range(parts):
                q = jnp.bitwise_xor(hid, j) if r else j
                pltpu.make_async_copy(pieces[r * parts + j], held.at[q], sems.at[q]).start()

    def copies(n, q):
        rows = pl.ds(pl.multiple_of(q * depth, depth), depth)
        there = pl.ds(pl.multiple_of(n * columns, 128), columns)
        return (
            pltpu.make_async_copy(gate_ref.at[expert, rows, there], gate_held.at[n, q], gate_sems.at[n, q]),
            pltpu.make_async_copy(up_ref.at[expert, rows, there], up_held.at[n, q], up_sems.at[n, q]),
        )

    @pl.loop(0, parts)
    def _(q):
        for copy in copies(0, q):
            copy.start()

    @pl.loop(0, parts)
    def _(q):
        pltpu.make_async_copy(pieces[0], held.at[q], sems.at[q]).wait()

    @pl.loop(0, chunks)
    def _(n):
        gate_sum[...] = jnp.zeros_like(gate_sum)
        up_sum[...] = jnp.zeros_like(up_sum)

        @pl.loop(0, parts)
        def _(q):
            @pl.when(n + 1 < chunks)
            def _():
                for copy in copies(n + 1, q):
                    copy.start()

            for copy in copies(n, q):
                copy.wait()
            gate_sum[...] += jnp.dot(held[q], gate_held[n, q], preferred_element_type=F32)
            up_sum[...] += jnp.dot(held[q], up_held[n, q], preferred_element_type=F32)

        gate = gate_sum[...]
        there = pl.ds(pl.multiple_of(n * columns, 128), columns)
        out_ref[:, there] = (gate / (1.0 + jnp.exp(-gate)) * up_sum[...]).astype(out_ref.dtype)


def gate_up(slot, info, pieces, gate_weight, up_weight):
    _, width, units = gate_weight.shape
    rows = pieces[0].shape[0]
    parts = len(pieces) // 4
    columns = tile_of(units, 256)
    held = pltpu.VMEM((units // columns, parts, width // parts, columns), BF16)
    total = pltpu.VMEM((rows, columns), F32)
    arrived = pltpu.SemaphoreType.DMA((units // columns, parts))
    anywhere = pl.BlockSpec(memory_space=pl.ANY)
    return pl.pallas_call(
        functools.partial(gate_up_kernel, slot, parts),
        in_specs=[pl.BlockSpec(memory_space=pltpu.SMEM)] + [anywhere] * (2 + len(pieces)),
        out_specs=pl.BlockSpec(memory_space=pltpu.VMEM),
        scratch_shapes=[
            pltpu.VMEM((parts, rows, width // parts), BF16),
            held,
            held,
            total,
            total,
            pltpu.SemaphoreType.DMA((parts,)),
            arrived,
            arrived,
        ],
        out_shape=jax.ShapeDtypeStruct((rows, units), BF16),
        compiler_params=params(),
        cost_estimate=pl.CostEstimate(
            flops=4 * rows * width * units,
            bytes_accessed=4 * width * units,
            transcendentals=rows * units,
        ),
        name="gate_up",
    )(info, *pieces, gate_weight, up_weight)


def down_kernel(slot, info, own, near, far, middle, end, weight_ref, combine_ref, routes, out_ref, held, weight_held, sems, weight_sems):
    block, expert, wid = info[slot, 0], info[slot, 1], info[8, 0]
    inner = (wid == 1) | (wid == 2)
    chunks, deep, units, columns = weight_held.shape

    for r, ref in enumerate((own, near, far)):
        pltpu.make_async_copy(ref, held.at[r], sems.at[r]).start()

    @pl.when(inner)
    def _():
        pltpu.make_async_copy(middle, held.at[3], sems.at[3]).start()

    @pl.when(jnp.logical_not(inner))
    def _():
        pltpu.make_async_copy(end, held.at[3], sems.at[3]).start()

    def weight_copy(n, r):
        rows = pl.ds(pl.multiple_of(jnp.bitwise_xor(wid, r) * units, units), units)
        there = pl.ds(pl.multiple_of(n * columns, 128), columns)
        return pltpu.make_async_copy(
            weight_ref.at[expert, rows, there], weight_held.at[n, r], weight_sems.at[n, r]
        )

    ahead = min(2, chunks)

    @pl.loop(0, ahead)
    def _(n):
        for r in range(deep):
            weight_copy(n, r).start()

    choices = combine_ref.shape[2]
    coef = sum(jnp.where(routes[block, c] == expert, combine_ref[block, :, c:c + 1], 0.0) for c in range(choices))
    for r in range(deep):
        pltpu.make_async_copy(own, held.at[r], sems.at[r]).wait()

    @pl.loop(0, chunks)
    def _(n):
        part = None
        for r in range(deep):
            weight_copy(n, r).wait()

            @pl.when(n + ahead < chunks)
            def _(r=r):
                weight_copy(n + ahead, r).start()

            more = jnp.dot(held[r], weight_held[n, r], preferred_element_type=F32)
            part = more if part is None else part + more
        there = pl.ds(pl.multiple_of(n * columns, 128), columns)
        out_ref[:, there] = coef * part


def down(slot, info, shards, combine, routes, down_weight):
    rows, units = shards[0].shape
    width = down_weight.shape[2]
    columns = tile_of(width, 256)
    near = pl.BlockSpec(memory_space=pltpu.VMEM)
    scalars = pl.BlockSpec(memory_space=pltpu.SMEM)
    return pl.pallas_call(
        functools.partial(down_kernel, slot),
        in_specs=[scalars] + [pl.BlockSpec(memory_space=pl.ANY)] * 6 + [near, scalars],
        out_specs=near,
        scratch_shapes=[
            pltpu.VMEM((4, rows, units), BF16),
            pltpu.VMEM((width // columns, 4, units, columns), BF16),
            pltpu.SemaphoreType.DMA((4,)),
            pltpu.SemaphoreType.DMA((width // columns, 4)),
        ],
        out_shape=jax.ShapeDtypeStruct((rows, width), F32),
        compiler_params=params(),
        cost_estimate=SHORT,
        name="down",
    )(info, *shards, down_weight, combine, routes)


FAR = [(0, 2), (2, 0), (1, 3), (3, 1)]
NEAR = [(0, 1), (1, 0), (2, 3), (3, 2)]
MIDDLE = [(1, 2), (2, 1)]
OUTWARD = [(1, 0), (2, 3)]
ACROSS = [(0, 2), (2, 0), (1, 3), (3, 1)]
TWIN = [(0, 1), (1, 0), (2, 3), (3, 2)]


def spread(tokens, wid, hid, *early):
    quarter = tokens.shape[1] // 4
    mine = lax.dynamic_slice_in_dim(tokens, hid * quarter, quarter, axis=1)
    far = lax.ppermute(mine, "wid", FAR)
    near = lax.ppermute(mine, "wid", NEAR)
    near_across = lax.ppermute(near, "hid", ACROSS)
    middle = lax.ppermute(after(mine, near), "wid", MIDDLE)
    outer = lax.ppermute(after(far, *early), "wid", OUTWARD)
    far_across = lax.ppermute(far, "hid", ACROSS)
    third = jnp.where((wid == 1) | (wid == 2), middle, outer)
    tokens = after(tokens, near)
    pieces = [tokens[:, q * quarter:(q + 1) * quarter] for q in range(4)]
    third_across = lax.ppermute(after(third, *pieces), "hid", ACROSS)
    for piece, across in ((near, near_across), (far, far_across), (third, third_across)):
        pieces += [piece, lax.ppermute(piece, "hid", TWIN), across, lax.ppermute(across, "hid", TWIN)]
    return pieces


def after(value, *done):
    return lax.optimization_barrier((value, *done))[0]


def sparse_device(tokens, gate_weight, up_weight, down_weight, routes, combine):
    experts = gate_weight.shape[0]
    blocks = routes.shape[0]
    rows = combine.shape[0] // blocks
    wid = lax.axis_index("wid")
    hid = lax.axis_index("hid")
    core, x = hid % 2, hid // 2
    info, number = named_pairs(experts, routes)
    count = number[0]
    combine = combine.reshape(blocks, rows, -1)
    pieces = spread(tokens, wid, hid, info, combine)

    def outward(hidden, near, far):
        middle = lax.ppermute(after(hidden, far), "wid", MIDDLE)
        outer = lax.ppermute(after(far, near), "wid", OUTWARD)
        return hidden, near, far, middle, outer

    def inward(hidden):
        return hidden, lax.ppermute(hidden, "wid", NEAR), lax.ppermute(hidden, "wid", FAR)

    def shares(parts, blocks):
        at = [2 * (1 - x) + 1 - core, 2 * (1 - x) + core, 2 * x + 1 - core, 2 * x + core]
        return [sum(jnp.where(block == b, part, 0.0) for part, block in zip(parts, blocks)) for b in at]

    def reduced(diagonal, across, twin, own):
        across = across + lax.ppermute(diagonal.astype(BF16), "hid", TWIN).astype(F32)
        own = own + lax.ppermute(twin.astype(BF16), "hid", TWIN).astype(F32)
        arriving = lax.ppermute(across.astype(BF16), "hid", ACROSS)
        return (lax.optimization_barrier(own) + arriving.astype(F32)).astype(BF16)

    most = 4

    def branch(slots, more):
        def run(info, combine, routes, *pieces):
            first, second, parts = [], [], []
            for slot in range(slots + 1):
                if slot < slots:
                    ready = info if slot < 2 else after(info, *first[slot - 2][1:])
                    hidden = gate_up(slot, ready, pieces, gate_weight, up_weight)
                    first.append(inward(after(hidden, first[-1][2]) if first else hidden))
                if slot >= 1:
                    hidden, near, far = first[slot - 1]
                    second.append(outward(hidden, near, after(far, parts[-1]) if parts else far))
                if slot >= 2:
                    ready = after(info, *first[slot - 1][1:], *(first[slot][:1] if slot < slots else ()))
                    parts.append(down(slot - 2, ready, second[slot - 2], combine, routes, down_weight))
            parts.append(down(slots - 1, info, second[slots - 1], combine, routes, down_weight))
            sums = shares(parts, [info[slot, 0] for slot in range(slots)])
            if more:

                def further(state):
                    at, *sums = state
                    one = jnp.concatenate([lax.dynamic_slice_in_dim(info, at, 1, axis=0), info[1:]], axis=0)
                    sent = outward(*inward(gate_up(0, one, pieces, gate_weight, up_weight)))
                    part = down(0, one, sent, combine, routes, down_weight)
                    return at + 1, *[old + new for old, new in zip(sums, shares([part], [one[0, 0]]))]

                _, *sums = lax.while_loop(lambda state: state[0] < count, further, (jnp.int32(slots), *sums))
            return reduced(*sums)

        return run

    branches = [branch(n + 1, False) for n in range(most)] + [branch(most, True)]
    return lax.switch(jnp.minimum(count, most + 1) - 1, branches, info, combine, routes, *pieces)


def dense_device(tokens, gate_weight, up_weight, down_weight, routes, combine):
    experts = gate_weight.shape[0]
    block = combine.shape[0] // routes.shape[0]
    rows_route = jnp.repeat(routes, block, axis=0)
    labels = jnp.arange(experts, dtype=jnp.int32)
    picked = (rows_route[:, :, None] == labels[None, None, :]).astype(F32)
    weights = jnp.sum(combine[:, :, None] * picked, axis=1)
    piece = lax.all_gather(tokens, "wid", axis=0, tiled=True)
    gate = jnp.einsum("td,edf->etf", piece, gate_weight, preferred_element_type=F32)
    upward = jnp.einsum("td,edf->etf", piece, up_weight, preferred_element_type=F32)
    hidden = (jax.nn.silu(gate) * upward).astype(BF16)
    summed = jnp.einsum(
        "etf,efd->etd",
        lax.all_gather(hidden, "wid", axis=2, tiled=True),
        down_weight,
        preferred_element_type=F32,
    )
    partial_value = jnp.sum(jnp.transpose(weights)[:, :, None] * summed, axis=0)
    own_rows = lax.psum_scatter(partial_value, "hid", scatter_dimension=0, tiled=True)
    return own_rows.astype(BF16)


def solution(mesh):
    placed = (
        P(("grp", "wid"), None),
        P(None, None, ("hid", "wid")),
        P(None, None, ("hid", "wid")),
        P(None, "hid", "wid"),
        P("grp", None),
        P("grp", None),
    )

    def program(tokens, gate_weight, up_weight, down_weight, routes, combine):
        blocks = routes.shape[0] // mesh.shape["grp"]
        square = mesh.shape["wid"] == 4 and mesh.shape["hid"] == 4 and blocks == 4
        return jax.shard_map(
            sparse_device if square else dense_device,
            mesh=mesh,
            in_specs=placed,
            out_specs=P(("grp", "hid"), "wid"),
            check_vma=False,
        )(tokens, gate_weight, up_weight, down_weight, routes, combine)

    return program
```

```python
import functools

import jax
import jax.numpy as jnp
from jax import lax
from jax.experimental import pallas as pl
from jax.experimental.pallas import tpu as pltpu
from jax.sharding import PartitionSpec as P

F32 = jnp.float32
BF16 = jnp.bfloat16
VMEM_LIMIT = 40 * 1024 * 1024


def tile_of(size, most):
    tile = min(size, most)
    while size % tile:
        tile -= 128
    return tile


def params():
    return pltpu.CompilerParams(vmem_limit_bytes=VMEM_LIMIT)


def named_kernel(experts, routes, info, number):
    blocks, choices = routes.shape
    slots = blocks * experts
    for slot in range(slots):
        for column in range(2 + choices):
            info[slot, column] = 0
    info[slots, 0] = lax.axis_index("wid")
    info[slots, 1] = lax.axis_index("hid")
    for choice in range(choices):
        info[slots, 2 + choice] = 0
    count = jnp.int32(0)
    for block in range(blocks):
        for expert in range(experts):
            named = routes[block, 0] == expert
            for choice in range(1, choices):
                named = named | (routes[block, choice] == expert)

            @pl.when(named)
            def _(block=block, expert=expert, count=count):
                info[count, 0] = block
                info[count, 1] = expert
                for choice in range(choices):
                    info[count, 2 + choice] = (routes[block, choice] == expert).astype(jnp.int32)

            count = count + named.astype(jnp.int32)
    number[0] = count


def named_pairs(experts, routes):
    scalars = pl.BlockSpec(memory_space=pltpu.SMEM)
    return pl.pallas_call(
        functools.partial(named_kernel, experts),
        in_specs=[scalars],
        out_specs=[scalars, scalars],
        out_shape=[
            jax.ShapeDtypeStruct((routes.shape[0] * experts + 1, 2 + routes.shape[1]), jnp.int32),
            jax.ShapeDtypeStruct((1,), jnp.int32),
        ],
        name="named",
    )(routes)


SHORT = pl.CostEstimate(flops=1000, bytes_accessed=1000, transcendentals=0)


def gate_up_kernel(slot, parts, info, *refs):
    pieces = refs[:4 * parts]
    gate_ref, up_ref, out_ref, held, gate_held, up_held, gate_sum, up_sum, sems, gate_sems, up_sems = refs[4 * parts:]
    chunks, _, depth, columns = gate_held.shape
    block, expert, wid, hid = info[slot, 0], info[slot, 1], info[8, 0], info[8, 1]
    away = jnp.bitwise_xor(block, wid)

    for r in range(4):
        @pl.when(away == r)
        def _(r=r):
            for j in range(parts):
                q = jnp.bitwise_xor(hid, j) if r else j
                pltpu.make_async_copy(pieces[r * parts + j], held.at[q], sems.at[q]).start()

    def copies(n, q):
        rows = pl.ds(pl.multiple_of(q * depth, depth), depth)
        there = pl.ds(pl.multiple_of(n * columns, 128), columns)
        return (
            pltpu.make_async_copy(gate_ref.at[expert, rows, there], gate_held.at[n, q], gate_sems.at[n, q]),
            pltpu.make_async_copy(up_ref.at[expert, rows, there], up_held.at[n, q], up_sems.at[n, q]),
        )

    @pl.loop(0, parts)
    def _(q):
        for copy in copies(0, q):
            copy.start()

    @pl.loop(0, parts)
    def _(q):
        pltpu.make_async_copy(pieces[0], held.at[q], sems.at[q]).wait()

    @pl.loop(0, chunks)
    def _(n):
        gate_sum[...] = jnp.zeros_like(gate_sum)
        up_sum[...] = jnp.zeros_like(up_sum)

        @pl.loop(0, parts)
        def _(q):
            @pl.when(n + 1 < chunks)
            def _():
                for copy in copies(n + 1, q):
                    copy.start()

            for copy in copies(n, q):
                copy.wait()
            gate_sum[...] += jnp.dot(held[q], gate_held[n, q], preferred_element_type=F32)
            up_sum[...] += jnp.dot(held[q], up_held[n, q], preferred_element_type=F32)

        gate = gate_sum[...]
        there = pl.ds(pl.multiple_of(n * columns, 128), columns)
        out_ref[:, there] = (gate / (1.0 + jnp.exp(-gate)) * up_sum[...]).astype(out_ref.dtype)


def gate_up(slot, info, pieces, gate_weight, up_weight):
    _, width, units = gate_weight.shape
    rows = pieces[0].shape[0]
    parts = len(pieces) // 4
    columns = tile_of(units, 256)
    held = pltpu.VMEM((units // columns, parts, width // parts, columns), BF16)
    total = pltpu.VMEM((rows, columns), F32)
    arrived = pltpu.SemaphoreType.DMA((units // columns, parts))
    anywhere = pl.BlockSpec(memory_space=pl.ANY)
    return pl.pallas_call(
        functools.partial(gate_up_kernel, slot, parts),
        in_specs=[pl.BlockSpec(memory_space=pltpu.SMEM)] + [anywhere] * (2 + len(pieces)),
        out_specs=pl.BlockSpec(memory_space=pltpu.VMEM),
        scratch_shapes=[
            pltpu.VMEM((parts, rows, width // parts), BF16),
            held,
            held,
            total,
            total,
            pltpu.SemaphoreType.DMA((parts,)),
            arrived,
            arrived,
        ],
        out_shape=jax.ShapeDtypeStruct((rows, units), BF16),
        compiler_params=params(),
        cost_estimate=pl.CostEstimate(
            flops=4 * rows * width * units,
            bytes_accessed=4 * width * units,
            transcendentals=rows * units,
        ),
        name="gate_up",
    )(info, *pieces, gate_weight, up_weight)


def down_kernel(slot, info, own, near, far, middle, end, weight_ref, combine_ref, out_ref, held, weight_held, sems, weight_sems):
    block, expert, wid = info[slot, 0], info[slot, 1], info[8, 0]
    inner = (wid == 1) | (wid == 2)
    chunks, deep, units, columns = weight_held.shape

    for r, ref in enumerate((own, near, far)):
        pltpu.make_async_copy(ref, held.at[r], sems.at[r]).start()

    @pl.when(inner)
    def _():
        pltpu.make_async_copy(middle, held.at[3], sems.at[3]).start()

    @pl.when(jnp.logical_not(inner))
    def _():
        pltpu.make_async_copy(end, held.at[3], sems.at[3]).start()

    def weight_copy(n, r):
        rows = pl.ds(pl.multiple_of(jnp.bitwise_xor(wid, r) * units, units), units)
        there = pl.ds(pl.multiple_of(n * columns, 128), columns)
        return pltpu.make_async_copy(
            weight_ref.at[expert, rows, there], weight_held.at[n, r], weight_sems.at[n, r]
        )

    ahead = min(2, chunks)

    @pl.loop(0, ahead)
    def _(n):
        for r in range(deep):
            weight_copy(n, r).start()

    choices = combine_ref.shape[2]
    coef = sum(jnp.where(info[slot, 2 + c] == 1, combine_ref[block, :, c:c + 1], 0.0) for c in range(choices))
    for r in range(deep):
        pltpu.make_async_copy(own, held.at[r], sems.at[r]).wait()

    @pl.loop(0, chunks)
    def _(n):
        part = None
        for r in range(deep):
            weight_copy(n, r).wait()

            @pl.when(n + ahead < chunks)
            def _(r=r):
                weight_copy(n + ahead, r).start()

            more = jnp.dot(held[r], weight_held[n, r], preferred_element_type=F32)
            part = more if part is None else part + more
        there = pl.ds(pl.multiple_of(n * columns, 128), columns)
        out_ref[:, there] = coef * part


def down(slot, info, shards, combine, down_weight):
    rows, units = shards[0].shape
    width = down_weight.shape[2]
    columns = tile_of(width, 256)
    near = pl.BlockSpec(memory_space=pltpu.VMEM)
    return pl.pallas_call(
        functools.partial(down_kernel, slot),
        in_specs=[pl.BlockSpec(memory_space=pltpu.SMEM)] + [pl.BlockSpec(memory_space=pl.ANY)] * 6 + [near],
        out_specs=near,
        scratch_shapes=[
            pltpu.VMEM((4, rows, units), BF16),
            pltpu.VMEM((width // columns, 4, units, columns), BF16),
            pltpu.SemaphoreType.DMA((4,)),
            pltpu.SemaphoreType.DMA((width // columns, 4)),
        ],
        out_shape=jax.ShapeDtypeStruct((rows, width), F32),
        compiler_params=params(),
        cost_estimate=SHORT,
        name="down",
    )(info, *shards, down_weight, combine)


FAR = [(0, 2), (2, 0), (1, 3), (3, 1)]
NEAR = [(0, 1), (1, 0), (2, 3), (3, 2)]
MIDDLE = [(1, 2), (2, 1)]
OUTWARD = [(1, 0), (2, 3)]
ACROSS = [(0, 2), (2, 0), (1, 3), (3, 1)]
TWIN = [(0, 1), (1, 0), (2, 3), (3, 2)]


def spread(tokens, wid, hid, *early):
    quarter = tokens.shape[1] // 4
    mine = lax.dynamic_slice_in_dim(tokens, hid * quarter, quarter, axis=1)
    far = lax.ppermute(mine, "wid", FAR)
    near = lax.ppermute(mine, "wid", NEAR)
    near_across = lax.ppermute(near, "hid", ACROSS)
    middle = lax.ppermute(mine, "wid", MIDDLE)
    far = after(far, near_across, *early)
    outer = lax.ppermute(far, "wid", OUTWARD)
    far_across = lax.ppermute(far, "hid", ACROSS)
    third = jnp.where((wid == 1) | (wid == 2), middle, outer)
    tokens = after(tokens, near)
    pieces = [tokens[:, q * quarter:(q + 1) * quarter] for q in range(4)]
    third_across = lax.ppermute(after(third, *pieces), "hid", ACROSS)
    for piece, across in ((near, near_across), (far, far_across), (third, third_across)):
        pieces += [piece, lax.ppermute(piece, "hid", TWIN), across, lax.ppermute(across, "hid", TWIN)]
    return pieces


def after(value, *done):
    return lax.optimization_barrier((value, *done))[0]


def sparse_device(tokens, gate_weight, up_weight, down_weight, routes, combine):
    experts = gate_weight.shape[0]
    blocks = routes.shape[0]
    rows = combine.shape[0] // blocks
    wid = lax.axis_index("wid")
    hid = lax.axis_index("hid")
    core, x = hid % 2, hid // 2
    info, number = named_pairs(experts, routes)
    count = number[0]
    combine = combine.reshape(blocks, rows, -1)
    pieces = spread(tokens, wid, hid, info, combine)

    def outward(hidden, near, far):
        middle = lax.ppermute(after(hidden, far), "wid", MIDDLE)
        outer = lax.ppermute(far, "wid", OUTWARD)
        return hidden, near, far, middle, outer

    def inward(hidden):
        return hidden, lax.ppermute(hidden, "wid", NEAR), lax.ppermute(hidden, "wid", FAR)

    def shares(parts, blocks):
        at = [2 * (1 - x) + 1 - core, 2 * (1 - x) + core, 2 * x + 1 - core, 2 * x + core]
        return [sum(jnp.where(block == b, part, 0.0) for part, block in zip(parts, blocks)) for b in at]

    def reduced(diagonal, across, twin, own):
        across = across + lax.ppermute(diagonal.astype(BF16), "hid", TWIN).astype(F32)
        own = own + lax.ppermute(twin.astype(BF16), "hid", TWIN).astype(F32)
        arriving = lax.ppermute(across.astype(BF16), "hid", ACROSS)
        return (lax.optimization_barrier(own) + arriving.astype(F32)).astype(BF16)

    most = 4

    def branch(slots, more):
        def run(info, combine, *pieces):
            first, second, parts = [], [], []
            for slot in range(slots + 1):
                if slot < slots:
                    ready = info if slot < 2 else after(info, *first[slot - 2][1:], *parts[-1:])
                    hidden = gate_up(slot, ready, pieces, gate_weight, up_weight)
                    first.append(inward(after(hidden, first[0][2]) if slot == 1 and slots == 2 else hidden))
                if slot >= 1:
                    hidden, near, far = first[slot - 1]
                    far = after(far, parts[-1]) if parts else after(far, near) if slots == 2 else far
                    second.append(outward(hidden, near, far))
                if slot >= 2:
                    ready = after(info, *first[slot - 1][1:], *(first[slot][:1] if slot < slots else ()))
                    parts.append(down(slot - 2, ready, second[slot - 2], combine, down_weight))
            parts.append(down(slots - 1, info, second[slots - 1], combine, down_weight))
            sums = shares(parts, [info[slot, 0] for slot in range(slots)])
            if more:

                def further(state):
                    at, *sums = state
                    one = jnp.concatenate([lax.dynamic_slice_in_dim(info, at, 1, axis=0), info[1:]], axis=0)
                    sent = outward(*inward(gate_up(0, one, pieces, gate_weight, up_weight)))
                    part = down(0, one, sent, combine, down_weight)
                    return at + 1, *[old + new for old, new in zip(sums, shares([part], [one[0, 0]]))]

                _, *sums = lax.while_loop(lambda state: state[0] < count, further, (jnp.int32(slots), *sums))
            return reduced(*sums)

        return run

    branches = [branch(n + 1, False) for n in range(most)] + [branch(most, True)]
    return lax.switch(jnp.minimum(count, most + 1) - 1, branches, info, combine, *pieces)


def dense_device(tokens, gate_weight, up_weight, down_weight, routes, combine):
    experts = gate_weight.shape[0]
    block = combine.shape[0] // routes.shape[0]
    rows_route = jnp.repeat(routes, block, axis=0)
    labels = jnp.arange(experts, dtype=jnp.int32)
    picked = (rows_route[:, :, None] == labels[None, None, :]).astype(F32)
    weights = jnp.sum(combine[:, :, None] * picked, axis=1)
    piece = lax.all_gather(tokens, "wid", axis=0, tiled=True)
    gate = jnp.einsum("td,edf->etf", piece, gate_weight, preferred_element_type=F32)
    upward = jnp.einsum("td,edf->etf", piece, up_weight, preferred_element_type=F32)
    hidden = (jax.nn.silu(gate) * upward).astype(BF16)
    summed = jnp.einsum(
        "etf,efd->etd",
        lax.all_gather(hidden, "wid", axis=2, tiled=True),
        down_weight,
        preferred_element_type=F32,
    )
    partial_value = jnp.sum(jnp.transpose(weights)[:, :, None] * summed, axis=0)
    own_rows = lax.psum_scatter(partial_value, "hid", scatter_dimension=0, tiled=True)
    return own_rows.astype(BF16)


def solution(mesh):
    placed = (
        P(("grp", "wid"), None),
        P(None, None, ("hid", "wid")),
        P(None, None, ("hid", "wid")),
        P(None, "hid", "wid"),
        P("grp", None),
        P("grp", None),
    )

    def program(tokens, gate_weight, up_weight, down_weight, routes, combine):
        blocks = routes.shape[0] // mesh.shape["grp"]
        square = mesh.shape["wid"] == 4 and mesh.shape["hid"] == 4 and blocks == 4
        return jax.shard_map(
            sparse_device if square else dense_device,
            mesh=mesh,
            in_specs=placed,
            out_specs=P(("grp", "hid"), "wid"),
            check_vma=False,
        )(tokens, gate_weight, up_weight, down_weight, routes, combine)

    return program
```

```python
import functools

import jax
import jax.numpy as jnp
from jax import lax
from jax.experimental import pallas as pl
from jax.experimental.pallas import tpu as pltpu
from jax.sharding import PartitionSpec as P

F32 = jnp.float32
BF16 = jnp.bfloat16
VMEM_LIMIT = 40 * 1024 * 1024


def tile_of(size, most):
    tile = min(size, most)
    while size % tile:
        tile -= 128
    return tile


def params():
    return pltpu.CompilerParams(vmem_limit_bytes=VMEM_LIMIT)


def named_kernel(experts, routes, info, number):
    blocks, choices = routes.shape
    slots = blocks * experts
    for slot in range(slots):
        for column in range(2 + choices):
            info[slot, column] = 0
    info[slots, 0] = lax.axis_index("wid")
    info[slots, 1] = lax.axis_index("hid")
    for choice in range(choices):
        info[slots, 2 + choice] = 0
    count = jnp.int32(0)
    for block in range(blocks):
        for expert in range(experts):
            named = routes[block, 0] == expert
            for choice in range(1, choices):
                named = named | (routes[block, choice] == expert)

            @pl.when(named)
            def _(block=block, expert=expert, count=count):
                info[count, 0] = block
                info[count, 1] = expert
                for choice in range(choices):
                    info[count, 2 + choice] = (routes[block, choice] == expert).astype(jnp.int32)

            count = count + named.astype(jnp.int32)
    number[0] = count


def named_pairs(experts, routes):
    scalars = pl.BlockSpec(memory_space=pltpu.SMEM)
    return pl.pallas_call(
        functools.partial(named_kernel, experts),
        in_specs=[scalars],
        out_specs=[scalars, scalars],
        out_shape=[
            jax.ShapeDtypeStruct((routes.shape[0] * experts + 1, 2 + routes.shape[1]), jnp.int32),
            jax.ShapeDtypeStruct((1,), jnp.int32),
        ],
        name="named",
    )(routes)


SHORT = pl.CostEstimate(flops=1000, bytes_accessed=1000, transcendentals=0)


def gate_up_kernel(slot, cuts, info, *refs):
    pieces = refs[:-11]
    gate_ref, up_ref, out_ref, held, gate_held, up_held, gate_sum, up_sum, sems, gate_sems, up_sems = refs[-11:]
    chunks, parts, depth, columns = gate_held.shape
    rows = held.shape[1]
    block, expert, wid, hid = info[slot, 0], info[slot, 1], info[8, 0], info[8, 1]
    away = jnp.bitwise_xor(block, wid)

    for r in range(4):
        @pl.when(away == r)
        def _(r=r):
            for j in range(parts):
                q = jnp.bitwise_xor(hid, j) if r else j
                for i in range(cuts[r]):
                    piece = pieces[parts * sum(cuts[:r]) + j * cuts[r] + i]
                    there = pl.ds(i * (rows // cuts[r]), rows // cuts[r])
                    pltpu.make_async_copy(piece, held.at[q, there], sems.at[q]).start()

    def copies(n, q):
        rows = pl.ds(pl.multiple_of(q * depth, depth), depth)
        there = pl.ds(pl.multiple_of(n * columns, 128), columns)
        return (
            pltpu.make_async_copy(gate_ref.at[expert, rows, there], gate_held.at[n, q], gate_sems.at[n, q]),
            pltpu.make_async_copy(up_ref.at[expert, rows, there], up_held.at[n, q], up_sems.at[n, q]),
        )

    @pl.loop(0, parts)
    def _(q):
        for copy in copies(0, q):
            copy.start()

    @pl.loop(0, parts)
    def _(q):
        pltpu.make_async_copy(pieces[0], held.at[q], sems.at[q]).wait()

    @pl.loop(0, chunks)
    def _(n):
        gate_sum[...] = jnp.zeros_like(gate_sum)
        up_sum[...] = jnp.zeros_like(up_sum)

        @pl.loop(0, parts)
        def _(q):
            @pl.when(n + 1 < chunks)
            def _():
                for copy in copies(n + 1, q):
                    copy.start()

            for copy in copies(n, q):
                copy.wait()
            gate_sum[...] += jnp.dot(held[q], gate_held[n, q], preferred_element_type=F32)
            up_sum[...] += jnp.dot(held[q], up_held[n, q], preferred_element_type=F32)

        gate = gate_sum[...]
        there = pl.ds(pl.multiple_of(n * columns, 128), columns)
        out_ref[:, there] = (gate / (1.0 + jnp.exp(-gate)) * up_sum[...]).astype(out_ref.dtype)


def gate_up(slot, info, pieces, gate_weight, up_weight):
    _, width, units = gate_weight.shape
    cuts = [len(blocks[0]) for blocks in pieces]
    parts = len(pieces[0])
    pieces = [cut for blocks in pieces for part in blocks for cut in part]
    rows = pieces[0].shape[0]
    columns = tile_of(units, 256)
    held = pltpu.VMEM((units // columns, parts, width // parts, columns), BF16)
    total = pltpu.VMEM((rows, columns), F32)
    arrived = pltpu.SemaphoreType.DMA((units // columns, parts))
    anywhere = pl.BlockSpec(memory_space=pl.ANY)
    return pl.pallas_call(
        functools.partial(gate_up_kernel, slot, cuts),
        in_specs=[pl.BlockSpec(memory_space=pltpu.SMEM)] + [anywhere] * (2 + len(pieces)),
        out_specs=pl.BlockSpec(memory_space=pltpu.VMEM),
        scratch_shapes=[
            pltpu.VMEM((parts, rows, width // parts), BF16),
            held,
            held,
            total,
            total,
            pltpu.SemaphoreType.DMA((parts,)),
            arrived,
            arrived,
        ],
        out_shape=jax.ShapeDtypeStruct((rows, units), BF16),
        compiler_params=params(),
        cost_estimate=pl.CostEstimate(
            flops=4 * rows * width * units,
            bytes_accessed=4 * width * units,
            transcendentals=rows * units,
        ),
        name="gate_up",
    )(info, *pieces, gate_weight, up_weight)


def down_kernel(slot, info, own, near, far, middle, end, weight_ref, combine_ref, out_ref, held, weight_held, sems, weight_sems):
    block, expert, wid = info[slot, 0], info[slot, 1], info[8, 0]
    inner = (wid == 1) | (wid == 2)
    chunks, deep, units, columns = weight_held.shape

    for r, ref in enumerate((own, near, far)):
        pltpu.make_async_copy(ref, held.at[r], sems.at[r]).start()

    @pl.when(inner)
    def _():
        pltpu.make_async_copy(middle, held.at[3], sems.at[3]).start()

    @pl.when(jnp.logical_not(inner))
    def _():
        pltpu.make_async_copy(end, held.at[3], sems.at[3]).start()

    def weight_copy(n, r):
        rows = pl.ds(pl.multiple_of(jnp.bitwise_xor(wid, r) * units, units), units)
        there = pl.ds(pl.multiple_of(n * columns, 128), columns)
        return pltpu.make_async_copy(
            weight_ref.at[expert, rows, there], weight_held.at[n, r], weight_sems.at[n, r]
        )

    ahead = min(2, chunks)

    @pl.loop(0, ahead)
    def _(n):
        for r in range(deep):
            weight_copy(n, r).start()

    choices = combine_ref.shape[2]
    coef = sum(jnp.where(info[slot, 2 + c] == 1, combine_ref[block, :, c:c + 1], 0.0) for c in range(choices))
    for r in range(deep):
        pltpu.make_async_copy(own, held.at[r], sems.at[r]).wait()

    @pl.loop(0, chunks)
    def _(n):
        part = None
        for r in range(deep):
            weight_copy(n, r).wait()

            @pl.when(n + ahead < chunks)
            def _(r=r):
                weight_copy(n + ahead, r).start()

            more = jnp.dot(held[r], weight_held[n, r], preferred_element_type=F32)
            part = more if part is None else part + more
        there = pl.ds(pl.multiple_of(n * columns, 128), columns)
        out_ref[:, there] = coef * part


def down(slot, info, shards, combine, down_weight):
    rows, units = shards[0].shape
    width = down_weight.shape[2]
    columns = tile_of(width, 256)
    near = pl.BlockSpec(memory_space=pltpu.VMEM)
    return pl.pallas_call(
        functools.partial(down_kernel, slot),
        in_specs=[pl.BlockSpec(memory_space=pltpu.SMEM)] + [pl.BlockSpec(memory_space=pl.ANY)] * 6 + [near],
        out_specs=near,
        scratch_shapes=[
            pltpu.VMEM((4, rows, units), BF16),
            pltpu.VMEM((width // columns, 4, units, columns), BF16),
            pltpu.SemaphoreType.DMA((4,)),
            pltpu.SemaphoreType.DMA((width // columns, 4)),
        ],
        out_shape=jax.ShapeDtypeStruct((rows, width), F32),
        compiler_params=params(),
        cost_estimate=SHORT,
        name="down",
    )(info, *shards, down_weight, combine)


FAR = [(0, 2), (2, 0), (1, 3), (3, 1)]
NEAR = [(0, 1), (1, 0), (2, 3), (3, 2)]
MIDDLE = [(1, 2), (2, 1)]
OUTWARD = [(1, 0), (2, 3)]
ACROSS = [(0, 2), (2, 0), (1, 3), (3, 1)]
TWIN = [(0, 1), (1, 0), (2, 3), (3, 2)]


def spread(tokens, wid, hid, *early):
    quarter = tokens.shape[1] // 4
    half = tokens.shape[0] // 2
    mine = lax.dynamic_slice_in_dim(tokens, hid * quarter, quarter, axis=1)
    upper = lax.ppermute(mine[:half], "wid", NEAR)
    far = lax.ppermute(mine, "wid", FAR)
    lower = lax.ppermute(after(mine[half:], upper), "wid", NEAR)
    upper_across = lax.ppermute(upper, "hid", ACROSS)
    tokens = after(tokens, upper)
    own = [tokens[:, q * quarter:(q + 1) * quarter] for q in range(4)]
    far = after(far, lower, upper_across, *early, *own)
    lower_across = lax.ppermute(lower, "hid", ACROSS)
    outer = lax.ppermute(far, "wid", OUTWARD)
    middle = lax.ppermute(after(mine, far), "wid", MIDDLE)
    far_across = lax.ppermute(far, "hid", ACROSS)
    third = jnp.where((wid == 1) | (wid == 2), middle, outer)
    third_across = lax.ppermute(after(third, lower_across), "hid", ACROSS)

    def parts(piece, across):
        return [piece, lax.ppermute(piece, "hid", TWIN), across, lax.ppermute(across, "hid", TWIN)]

    halves = zip(parts(upper, upper_across), parts(lower, lower_across))
    return [
        [(piece,) for piece in own],
        list(halves),
        [(piece,) for piece in parts(far, far_across)],
        [(piece,) for piece in parts(third, third_across)],
    ]


def after(value, *done):
    return lax.optimization_barrier((value, *done))[0]


def sparse_device(tokens, gate_weight, up_weight, down_weight, routes, combine):
    experts = gate_weight.shape[0]
    blocks = routes.shape[0]
    rows = combine.shape[0] // blocks
    wid = lax.axis_index("wid")
    hid = lax.axis_index("hid")
    core, x = hid % 2, hid // 2
    info, number = named_pairs(experts, routes)
    count = number[0]
    combine = combine.reshape(blocks, rows, -1)
    pieces = spread(tokens, wid, hid, info, combine)

    def outward(hidden, near, far):
        middle = lax.ppermute(after(hidden, far), "wid", MIDDLE)
        outer = lax.ppermute(far, "wid", OUTWARD)
        return hidden, near, far, middle, outer

    def inward(hidden):
        return hidden, lax.ppermute(hidden, "wid", NEAR), lax.ppermute(hidden, "wid", FAR)

    def shares(parts, blocks):
        at = [2 * (1 - x) + 1 - core, 2 * (1 - x) + core, 2 * x + 1 - core, 2 * x + core]
        return [sum(jnp.where(block == b, part, 0.0) for part, block in zip(parts, blocks)) for b in at]

    def reduced(diagonal, across, twin, own):
        across = across + lax.ppermute(diagonal.astype(BF16), "hid", TWIN).astype(F32)
        own = own + lax.ppermute(twin.astype(BF16), "hid", TWIN).astype(F32)
        arriving = lax.ppermute(across.astype(BF16), "hid", ACROSS)
        return (lax.optimization_barrier(own) + arriving.astype(F32)).astype(BF16)

    most = 4

    def branch(slots, more):
        def run(info, combine, pieces):
            first, second, parts = [], [], []
            for slot in range(slots + 1):
                if slot < slots:
                    ready = info if slot < 2 else after(info, *first[slot - 2][1:], *parts[-1:])
                    hidden = gate_up(slot, ready, pieces, gate_weight, up_weight)
                    first.append(inward(after(hidden, first[0][2]) if slot == 1 and slots == 2 else hidden))
                if slot >= 1:
                    hidden, near, far = first[slot - 1]
                    far = after(far, parts[-1]) if parts else after(far, near) if slots == 2 else far
                    second.append(outward(hidden, near, far))
                if slot >= 2:
                    ready = after(info, *first[slot - 1][1:], *(first[slot][:1] if slot < slots else ()))
                    parts.append(down(slot - 2, ready, second[slot - 2], combine, down_weight))
            parts.append(down(slots - 1, info, second[slots - 1], combine, down_weight))
            sums = shares(parts, [info[slot, 0] for slot in range(slots)])
            if more:

                def further(state):
                    at, *sums = state
                    one = jnp.concatenate([lax.dynamic_slice_in_dim(info, at, 1, axis=0), info[1:]], axis=0)
                    sent = outward(*inward(gate_up(0, one, pieces, gate_weight, up_weight)))
                    part = down(0, one, sent, combine, down_weight)
                    return at + 1, *[old + new for old, new in zip(sums, shares([part], [one[0, 0]]))]

                _, *sums = lax.while_loop(lambda state: state[0] < count, further, (jnp.int32(slots), *sums))
            return reduced(*sums)

        return run

    branches = [branch(n + 1, False) for n in range(most)] + [branch(most, True)]
    return lax.switch(jnp.minimum(count, most + 1) - 1, branches, info, combine, pieces)


def dense_device(tokens, gate_weight, up_weight, down_weight, routes, combine):
    experts = gate_weight.shape[0]
    block = combine.shape[0] // routes.shape[0]
    rows_route = jnp.repeat(routes, block, axis=0)
    labels = jnp.arange(experts, dtype=jnp.int32)
    picked = (rows_route[:, :, None] == labels[None, None, :]).astype(F32)
    weights = jnp.sum(combine[:, :, None] * picked, axis=1)
    piece = lax.all_gather(tokens, "wid", axis=0, tiled=True)
    gate = jnp.einsum("td,edf->etf", piece, gate_weight, preferred_element_type=F32)
    upward = jnp.einsum("td,edf->etf", piece, up_weight, preferred_element_type=F32)
    hidden = (jax.nn.silu(gate) * upward).astype(BF16)
    summed = jnp.einsum(
        "etf,efd->etd",
        lax.all_gather(hidden, "wid", axis=2, tiled=True),
        down_weight,
        preferred_element_type=F32,
    )
    partial_value = jnp.sum(jnp.transpose(weights)[:, :, None] * summed, axis=0)
    own_rows = lax.psum_scatter(partial_value, "hid", scatter_dimension=0, tiled=True)
    return own_rows.astype(BF16)


def solution(mesh):
    placed = (
        P(("grp", "wid"), None),
        P(None, None, ("hid", "wid")),
        P(None, None, ("hid", "wid")),
        P(None, "hid", "wid"),
        P("grp", None),
        P("grp", None),
    )

    def program(tokens, gate_weight, up_weight, down_weight, routes, combine):
        blocks = routes.shape[0] // mesh.shape["grp"]
        square = mesh.shape["wid"] == 4 and mesh.shape["hid"] == 4 and blocks == 4
        return jax.shard_map(
            sparse_device if square else dense_device,
            mesh=mesh,
            in_specs=placed,
            out_specs=P(("grp", "hid"), "wid"),
            check_vma=False,
        )(tokens, gate_weight, up_weight, down_weight, routes, combine)

    return program
```

```python
import functools

import jax
import jax.numpy as jnp
from jax import lax
from jax.experimental import pallas as pl
from jax.experimental.pallas import tpu as pltpu
from jax.sharding import PartitionSpec as P

F32 = jnp.float32
BF16 = jnp.bfloat16
VMEM_LIMIT = 40 * 1024 * 1024


def tile_of(size, most):
    tile = min(size, most)
    while size % tile:
        tile -= 128
    return tile


def params():
    return pltpu.CompilerParams(vmem_limit_bytes=VMEM_LIMIT)


def named_kernel(experts, routes, info, number):
    blocks, choices = routes.shape
    slots = blocks * experts
    for slot in range(slots):
        for column in range(2 + choices):
            info[slot, column] = 0
    info[slots, 0] = lax.axis_index("wid")
    info[slots, 1] = lax.axis_index("hid")
    for choice in range(choices):
        info[slots, 2 + choice] = 0
    count = jnp.int32(0)
    for block in range(blocks):
        for expert in range(experts):
            named = routes[block, 0] == expert
            for choice in range(1, choices):
                named = named | (routes[block, choice] == expert)

            @pl.when(named)
            def _(block=block, expert=expert, count=count):
                info[count, 0] = block
                info[count, 1] = expert
                for choice in range(choices):
                    info[count, 2 + choice] = (routes[block, choice] == expert).astype(jnp.int32)

            count = count + named.astype(jnp.int32)
    number[0] = count


def named_pairs(experts, routes):
    scalars = pl.BlockSpec(memory_space=pltpu.SMEM)
    return pl.pallas_call(
        functools.partial(named_kernel, experts),
        in_specs=[scalars],
        out_specs=[scalars, scalars],
        out_shape=[
            jax.ShapeDtypeStruct((routes.shape[0] * experts + 1, 2 + routes.shape[1]), jnp.int32),
            jax.ShapeDtypeStruct((1,), jnp.int32),
        ],
        name="named",
    )(routes)


SHORT = pl.CostEstimate(flops=1000, bytes_accessed=1000, transcendentals=0)


def gate_up_kernel(slot, cuts, info, *refs):
    pieces = refs[:-11]
    gate_ref, up_ref, out_ref, held, gate_held, up_held, gate_sum, up_sum, sems, gate_sems, up_sems = refs[-11:]
    chunks, parts, depth, columns = gate_held.shape
    rows = held.shape[1]
    block, expert, wid, hid = info[slot, 0], info[slot, 1], info[8, 0], info[8, 1]
    away = jnp.bitwise_xor(block, wid)

    for r in range(4):
        @pl.when(away == r)
        def _(r=r):
            for j in range(parts):
                q = jnp.bitwise_xor(hid, j) if r else j
                for i in range(cuts[r]):
                    piece = pieces[parts * sum(cuts[:r]) + j * cuts[r] + i]
                    there = pl.ds(i * (rows // cuts[r]), rows // cuts[r])
                    pltpu.make_async_copy(piece, held.at[q, there], sems.at[q]).start()

    def copies(n, q):
        rows = pl.ds(pl.multiple_of(q * depth, depth), depth)
        there = pl.ds(pl.multiple_of(n * columns, 128), columns)
        return (
            pltpu.make_async_copy(gate_ref.at[expert, rows, there], gate_held.at[n, q], gate_sems.at[n, q]),
            pltpu.make_async_copy(up_ref.at[expert, rows, there], up_held.at[n, q], up_sems.at[n, q]),
        )

    @pl.loop(0, parts)
    def _(q):
        for copy in copies(0, q):
            copy.start()

    @pl.loop(0, parts)
    def _(q):
        pltpu.make_async_copy(pieces[0], held.at[q], sems.at[q]).wait()

    @pl.loop(0, chunks)
    def _(n):
        gate_sum[...] = jnp.zeros_like(gate_sum)
        up_sum[...] = jnp.zeros_like(up_sum)

        @pl.loop(0, parts)
        def _(q):
            @pl.when(n + 1 < chunks)
            def _():
                for copy in copies(n + 1, q):
                    copy.start()

            for copy in copies(n, q):
                copy.wait()
            gate_sum[...] += jnp.dot(held[q], gate_held[n, q], preferred_element_type=F32)
            up_sum[...] += jnp.dot(held[q], up_held[n, q], preferred_element_type=F32)

        gate = gate_sum[...]
        there = pl.ds(pl.multiple_of(n * columns, 128), columns)
        out_ref[:, there] = (gate / (1.0 + jnp.exp(-gate)) * up_sum[...]).astype(out_ref.dtype)


def gate_up(slot, info, pieces, gate_weight, up_weight):
    _, width, units = gate_weight.shape
    cuts = [len(blocks[0]) for blocks in pieces]
    parts = len(pieces[0])
    pieces = [cut for blocks in pieces for part in blocks for cut in part]
    rows = pieces[0].shape[0]
    columns = tile_of(units, 256)
    held = pltpu.VMEM((units // columns, parts, width // parts, columns), BF16)
    total = pltpu.VMEM((rows, columns), F32)
    arrived = pltpu.SemaphoreType.DMA((units // columns, parts))
    anywhere = pl.BlockSpec(memory_space=pl.ANY)
    return pl.pallas_call(
        functools.partial(gate_up_kernel, slot, cuts),
        in_specs=[pl.BlockSpec(memory_space=pltpu.SMEM)] + [anywhere] * (2 + len(pieces)),
        out_specs=pl.BlockSpec(memory_space=pltpu.VMEM),
        scratch_shapes=[
            pltpu.VMEM((parts, rows, width // parts), BF16),
            held,
            held,
            total,
            total,
            pltpu.SemaphoreType.DMA((parts,)),
            arrived,
            arrived,
        ],
        out_shape=jax.ShapeDtypeStruct((rows, units), BF16),
        compiler_params=params(),
        cost_estimate=pl.CostEstimate(
            flops=4 * rows * width * units,
            bytes_accessed=4 * width * units,
            transcendentals=rows * units,
        ),
        name="gate_up",
    )(info, *pieces, gate_weight, up_weight)


def down_kernel(slot, info, own, near, far, middle, end, weight_ref, combine_ref, out_ref, held, weight_held, sems, weight_sems):
    block, expert, wid = info[slot, 0], info[slot, 1], info[8, 0]
    inner = (wid == 1) | (wid == 2)
    chunks, deep, units, columns = weight_held.shape

    for r, ref in enumerate((own, near, far)):
        pltpu.make_async_copy(ref, held.at[r], sems.at[r]).start()

    @pl.when(inner)
    def _():
        pltpu.make_async_copy(middle, held.at[3], sems.at[3]).start()

    @pl.when(jnp.logical_not(inner))
    def _():
        pltpu.make_async_copy(end, held.at[3], sems.at[3]).start()

    def weight_copy(n, r):
        rows = pl.ds(pl.multiple_of(jnp.bitwise_xor(wid, r) * units, units), units)
        there = pl.ds(pl.multiple_of(n * columns, 128), columns)
        return pltpu.make_async_copy(
            weight_ref.at[expert, rows, there], weight_held.at[n, r], weight_sems.at[n, r]
        )

    ahead = min(2, chunks)

    @pl.loop(0, ahead)
    def _(n):
        for r in range(deep):
            weight_copy(n, r).start()

    choices = combine_ref.shape[2]
    coef = sum(jnp.where(info[slot, 2 + c] == 1, combine_ref[block, :, c:c + 1], 0.0) for c in range(choices))
    for r in range(deep):
        pltpu.make_async_copy(own, held.at[r], sems.at[r]).wait()

    @pl.loop(0, chunks)
    def _(n):
        part = None
        for r in range(deep):
            weight_copy(n, r).wait()

            @pl.when(n + ahead < chunks)
            def _(r=r):
                weight_copy(n + ahead, r).start()

            more = jnp.dot(held[r], weight_held[n, r], preferred_element_type=F32)
            part = more if part is None else part + more
        there = pl.ds(pl.multiple_of(n * columns, 128), columns)
        out_ref[:, there] = coef * part


def down(slot, info, shards, combine, down_weight):
    rows, units = shards[0].shape
    width = down_weight.shape[2]
    columns = tile_of(width, 256)
    near = pl.BlockSpec(memory_space=pltpu.VMEM)
    return pl.pallas_call(
        functools.partial(down_kernel, slot),
        in_specs=[pl.BlockSpec(memory_space=pltpu.SMEM)] + [pl.BlockSpec(memory_space=pl.ANY)] * 6 + [near],
        out_specs=near,
        scratch_shapes=[
            pltpu.VMEM((4, rows, units), BF16),
            pltpu.VMEM((width // columns, 4, units, columns), BF16),
            pltpu.SemaphoreType.DMA((4,)),
            pltpu.SemaphoreType.DMA((width // columns, 4)),
        ],
        out_shape=jax.ShapeDtypeStruct((rows, width), F32),
        compiler_params=params(),
        cost_estimate=SHORT,
        name="down",
    )(info, *shards, down_weight, combine)


FAR = [(0, 2), (2, 0), (1, 3), (3, 1)]
NEAR = [(0, 1), (1, 0), (2, 3), (3, 2)]
MIDDLE = [(1, 2), (2, 1)]
OUTWARD = [(1, 0), (2, 3)]
ACROSS = [(0, 2), (2, 0), (1, 3), (3, 1)]
TWIN = [(0, 1), (1, 0), (2, 3), (3, 2)]


def spread(tokens, wid, hid, *early):
    quarter = tokens.shape[1] // 4
    half = tokens.shape[0] // 2
    mine = lax.dynamic_slice_in_dim(tokens, hid * quarter, quarter, axis=1)
    upper = lax.ppermute(mine[:half], "wid", NEAR)
    far = lax.ppermute(mine, "wid", FAR)
    lower = lax.ppermute(after(mine[half:], upper), "wid", NEAR)
    upper_across = lax.ppermute(upper, "hid", ACROSS)
    tokens = after(tokens, upper)
    own = [tokens[:, q * quarter:(q + 1) * quarter] for q in range(4)]
    lower_across = lax.ppermute(lower, "hid", ACROSS)
    far = after(far, upper_across, lower_across, *early, *own)
    outer = lax.ppermute(far, "wid", OUTWARD)
    middle = lax.ppermute(after(mine, far), "wid", MIDDLE)
    far_across = lax.ppermute(far, "hid", ACROSS)
    third = jnp.where((wid == 1) | (wid == 2), middle, outer)
    third_across = lax.ppermute(third, "hid", ACROSS)

    def parts(piece, across):
        return [piece, lax.ppermute(piece, "hid", TWIN), across, lax.ppermute(across, "hid", TWIN)]

    halves = zip(parts(upper, upper_across), parts(lower, lower_across))
    return [
        [(piece,) for piece in own],
        list(halves),
        [(piece,) for piece in parts(far, far_across)],
        [(piece,) for piece in parts(third, third_across)],
    ]


def after(value, *done):
    return lax.optimization_barrier((value, *done))[0]


def sparse_device(tokens, gate_weight, up_weight, down_weight, routes, combine):
    experts = gate_weight.shape[0]
    blocks = routes.shape[0]
    rows = combine.shape[0] // blocks
    wid = lax.axis_index("wid")
    hid = lax.axis_index("hid")
    core, x = hid % 2, hid // 2
    info, number = named_pairs(experts, routes)
    count = number[0]
    combine = combine.reshape(blocks, rows, -1)
    pieces = spread(tokens, wid, hid, info, combine)

    def outward(hidden, near, far):
        middle = lax.ppermute(after(hidden, far), "wid", MIDDLE)
        outer = lax.ppermute(far, "wid", OUTWARD)
        return hidden, near, far, middle, outer

    def inward(hidden):
        return hidden, lax.ppermute(hidden, "wid", NEAR), lax.ppermute(hidden, "wid", FAR)

    def shares(parts, blocks):
        at = [2 * (1 - x) + 1 - core, 2 * (1 - x) + core, 2 * x + 1 - core, 2 * x + core]
        return [sum(jnp.where(block == b, part, 0.0) for part, block in zip(parts, blocks)) for b in at]

    def reduced(diagonal, across, twin, own):
        across = across + lax.ppermute(diagonal.astype(BF16), "hid", TWIN).astype(F32)
        own = own + lax.ppermute(twin.astype(BF16), "hid", TWIN).astype(F32)
        arriving = lax.ppermute(across.astype(BF16), "hid", ACROSS)
        return (lax.optimization_barrier(own) + arriving.astype(F32)).astype(BF16)

    most = 4

    def branch(slots, more):
        def run(info, combine, pieces):
            first, second, parts = [], [], []
            for slot in range(slots + 1):
                if slot < slots:
                    ready = info if slot < 2 else after(info, *first[slot - 2][1:], *parts[-1:])
                    hidden = gate_up(slot, ready, pieces, gate_weight, up_weight)
                    first.append(inward(after(hidden, first[0][2]) if slot == 1 and slots == 2 else hidden))
                if slot >= 1:
                    hidden, near, far = first[slot - 1]
                    far = after(far, parts[-1]) if parts else after(far, near) if slots == 2 else far
                    second.append(outward(hidden, near, far))
                if slot >= 2:
                    ready = after(info, *first[slot - 1][1:], *(first[slot][:1] if slot < slots else ()))
                    parts.append(down(slot - 2, ready, second[slot - 2], combine, down_weight))
            parts.append(down(slots - 1, info, second[slots - 1], combine, down_weight))
            sums = shares(parts, [info[slot, 0] for slot in range(slots)])
            if more:

                def further(state):
                    at, *sums = state
                    one = jnp.concatenate([lax.dynamic_slice_in_dim(info, at, 1, axis=0), info[1:]], axis=0)
                    sent = outward(*inward(gate_up(0, one, pieces, gate_weight, up_weight)))
                    part = down(0, one, sent, combine, down_weight)
                    return at + 1, *[old + new for old, new in zip(sums, shares([part], [one[0, 0]]))]

                _, *sums = lax.while_loop(lambda state: state[0] < count, further, (jnp.int32(slots), *sums))
            return reduced(*sums)

        return run

    branches = [branch(n + 1, False) for n in range(most)] + [branch(most, True)]
    return lax.switch(jnp.minimum(count, most + 1) - 1, branches, info, combine, pieces)


def dense_device(tokens, gate_weight, up_weight, down_weight, routes, combine):
    experts = gate_weight.shape[0]
    block = combine.shape[0] // routes.shape[0]
    rows_route = jnp.repeat(routes, block, axis=0)
    labels = jnp.arange(experts, dtype=jnp.int32)
    picked = (rows_route[:, :, None] == labels[None, None, :]).astype(F32)
    weights = jnp.sum(combine[:, :, None] * picked, axis=1)
    piece = lax.all_gather(tokens, "wid", axis=0, tiled=True)
    gate = jnp.einsum("td,edf->etf", piece, gate_weight, preferred_element_type=F32)
    upward = jnp.einsum("td,edf->etf", piece, up_weight, preferred_element_type=F32)
    hidden = (jax.nn.silu(gate) * upward).astype(BF16)
    summed = jnp.einsum(
        "etf,efd->etd",
        lax.all_gather(hidden, "wid", axis=2, tiled=True),
        down_weight,
        preferred_element_type=F32,
    )
    partial_value = jnp.sum(jnp.transpose(weights)[:, :, None] * summed, axis=0)
    own_rows = lax.psum_scatter(partial_value, "hid", scatter_dimension=0, tiled=True)
    return own_rows.astype(BF16)


def solution(mesh):
    placed = (
        P(("grp", "wid"), None),
        P(None, None, ("hid", "wid")),
        P(None, None, ("hid", "wid")),
        P(None, "hid", "wid"),
        P("grp", None),
        P("grp", None),
    )

    def program(tokens, gate_weight, up_weight, down_weight, routes, combine):
        blocks = routes.shape[0] // mesh.shape["grp"]
        square = mesh.shape["wid"] == 4 and mesh.shape["hid"] == 4 and blocks == 4
        return jax.shard_map(
            sparse_device if square else dense_device,
            mesh=mesh,
            in_specs=placed,
            out_specs=P(("grp", "hid"), "wid"),
            check_vma=False,
        )(tokens, gate_weight, up_weight, down_weight, routes, combine)

    return program
```

```python
import functools

import jax
import jax.numpy as jnp
from jax import lax
from jax.experimental import pallas as pl
from jax.experimental.pallas import tpu as pltpu
from jax.sharding import PartitionSpec as P

F32 = jnp.float32
BF16 = jnp.bfloat16
VMEM_LIMIT = 40 * 1024 * 1024


def tile_of(size, most):
    tile = min(size, most)
    while size % tile:
        tile -= 128
    return tile


def params():
    return pltpu.CompilerParams(vmem_limit_bytes=VMEM_LIMIT)


def named_kernel(experts, routes, info, number):
    blocks, choices = routes.shape
    slots = blocks * experts
    for slot in range(slots):
        for column in range(2 + choices):
            info[slot, column] = 0
    info[slots, 0] = lax.axis_index("wid")
    info[slots, 1] = lax.axis_index("hid")
    for choice in range(choices):
        info[slots, 2 + choice] = 0
    count = jnp.int32(0)
    for block in range(blocks):
        for expert in range(experts):
            named = routes[block, 0] == expert
            for choice in range(1, choices):
                named = named | (routes[block, choice] == expert)

            @pl.when(named)
            def _(block=block, expert=expert, count=count):
                info[count, 0] = block
                info[count, 1] = expert
                for choice in range(choices):
                    info[count, 2 + choice] = (routes[block, choice] == expert).astype(jnp.int32)

            count = count + named.astype(jnp.int32)
    number[0] = count


def named_pairs(experts, routes):
    scalars = pl.BlockSpec(memory_space=pltpu.SMEM)
    return pl.pallas_call(
        functools.partial(named_kernel, experts),
        in_specs=[scalars],
        out_specs=[scalars, scalars],
        out_shape=[
            jax.ShapeDtypeStruct((routes.shape[0] * experts + 1, 2 + routes.shape[1]), jnp.int32),
            jax.ShapeDtypeStruct((1,), jnp.int32),
        ],
        name="named",
    )(routes)


SHORT = pl.CostEstimate(flops=1000, bytes_accessed=1000, transcendentals=0)


def gate_up_kernel(slot, parts, info, *refs):
    pieces = refs[:4 * parts]
    gate_ref, up_ref, out_ref, held, gate_held, up_held, gate_sum, up_sum, sems, gate_sems, up_sems = refs[4 * parts:]
    chunks, _, depth, columns = gate_held.shape
    block, expert, wid, hid = info[slot, 0], info[slot, 1], info[8, 0], info[8, 1]
    away = jnp.bitwise_xor(block, wid)

    for r in range(4):
        @pl.when(away == r)
        def _(r=r):
            for j in range(parts):
                q = jnp.bitwise_xor(hid, j) if r else j
                pltpu.make_async_copy(pieces[r * parts + j], held.at[q], sems.at[q]).start()

    def copies(n, q):
        rows = pl.ds(pl.multiple_of(q * depth, depth), depth)
        there = pl.ds(pl.multiple_of(n * columns, 128), columns)
        return (
            pltpu.make_async_copy(gate_ref.at[expert, rows, there], gate_held.at[n, q], gate_sems.at[n, q]),
            pltpu.make_async_copy(up_ref.at[expert, rows, there], up_held.at[n, q], up_sems.at[n, q]),
        )

    @pl.loop(0, parts)
    def _(q):
        for copy in copies(0, q):
            copy.start()

    @pl.loop(0, parts)
    def _(q):
        pltpu.make_async_copy(pieces[0], held.at[q], sems.at[q]).wait()

    @pl.loop(0, chunks)
    def _(n):
        gate_sum[...] = jnp.zeros_like(gate_sum)
        up_sum[...] = jnp.zeros_like(up_sum)

        @pl.loop(0, parts)
        def _(q):
            @pl.when(n + 1 < chunks)
            def _():
                for copy in copies(n + 1, q):
                    copy.start()

            for copy in copies(n, q):
                copy.wait()
            gate_sum[...] += jnp.dot(held[q], gate_held[n, q], preferred_element_type=F32)
            up_sum[...] += jnp.dot(held[q], up_held[n, q], preferred_element_type=F32)

        gate = gate_sum[...]
        there = pl.ds(pl.multiple_of(n * columns, 128), columns)
        out_ref[:, there] = (gate / (1.0 + jnp.exp(-gate)) * up_sum[...]).astype(out_ref.dtype)


def gate_up(slot, info, pieces, gate_weight, up_weight):
    _, width, units = gate_weight.shape
    rows = pieces[0].shape[0]
    parts = len(pieces) // 4
    columns = tile_of(units, 256)
    held = pltpu.VMEM((units // columns, parts, width // parts, columns), BF16)
    total = pltpu.VMEM((rows, columns), F32)
    arrived = pltpu.SemaphoreType.DMA((units // columns, parts))
    anywhere = pl.BlockSpec(memory_space=pl.ANY)
    return pl.pallas_call(
        functools.partial(gate_up_kernel, slot, parts),
        in_specs=[pl.BlockSpec(memory_space=pltpu.SMEM)] + [anywhere] * (2 + len(pieces)),
        out_specs=pl.BlockSpec(memory_space=pltpu.VMEM),
        scratch_shapes=[
            pltpu.VMEM((parts, rows, width // parts), BF16),
            held,
            held,
            total,
            total,
            pltpu.SemaphoreType.DMA((parts,)),
            arrived,
            arrived,
        ],
        out_shape=jax.ShapeDtypeStruct((rows, units), BF16),
        compiler_params=params(),
        cost_estimate=pl.CostEstimate(
            flops=4 * rows * width * units,
            bytes_accessed=4 * width * units,
            transcendentals=rows * units,
        ),
        name="gate_up",
    )(info, *pieces, gate_weight, up_weight)


def down_kernel(slot, info, own, near, far, middle, end, weight_ref, combine_ref, out_ref, held, weight_held, sems, weight_sems):
    block, expert, wid = info[slot, 0], info[slot, 1], info[8, 0]
    inner = (wid == 1) | (wid == 2)
    chunks, deep, units, columns = weight_held.shape

    for r, ref in enumerate((own, near, far)):
        pltpu.make_async_copy(ref, held.at[r], sems.at[r]).start()

    @pl.when(inner)
    def _():
        pltpu.make_async_copy(middle, held.at[3], sems.at[3]).start()

    @pl.when(jnp.logical_not(inner))
    def _():
        pltpu.make_async_copy(end, held.at[3], sems.at[3]).start()

    def weight_copy(n, r):
        rows = pl.ds(pl.multiple_of(jnp.bitwise_xor(wid, r) * units, units), units)
        there = pl.ds(pl.multiple_of(n * columns, 128), columns)
        return pltpu.make_async_copy(
            weight_ref.at[expert, rows, there], weight_held.at[n, r], weight_sems.at[n, r]
        )

    ahead = min(2, chunks)

    @pl.loop(0, ahead)
    def _(n):
        for r in range(deep):
            weight_copy(n, r).start()

    choices = combine_ref.shape[2]
    coef = sum(jnp.where(info[slot, 2 + c] == 1, combine_ref[block, :, c:c + 1], 0.0) for c in range(choices))
    for r in range(deep):
        pltpu.make_async_copy(own, held.at[r], sems.at[r]).wait()

    @pl.loop(0, chunks)
    def _(n):
        part = None
        for r in range(deep):
            weight_copy(n, r).wait()

            @pl.when(n + ahead < chunks)
            def _(r=r):
                weight_copy(n + ahead, r).start()

            more = jnp.dot(held[r], weight_held[n, r], preferred_element_type=F32)
            part = more if part is None else part + more
        there = pl.ds(pl.multiple_of(n * columns, 128), columns)
        out_ref[:, there] = coef * part


def down(slot, info, shards, combine, down_weight):
    rows, units = shards[0].shape
    width = down_weight.shape[2]
    columns = tile_of(width, 256)
    near = pl.BlockSpec(memory_space=pltpu.VMEM)
    return pl.pallas_call(
        functools.partial(down_kernel, slot),
        in_specs=[pl.BlockSpec(memory_space=pltpu.SMEM)] + [pl.BlockSpec(memory_space=pl.ANY)] * 6 + [near],
        out_specs=near,
        scratch_shapes=[
            pltpu.VMEM((4, rows, units), BF16),
            pltpu.VMEM((width // columns, 4, units, columns), BF16),
            pltpu.SemaphoreType.DMA((4,)),
            pltpu.SemaphoreType.DMA((width // columns, 4)),
        ],
        out_shape=jax.ShapeDtypeStruct((rows, width), F32),
        compiler_params=params(),
        cost_estimate=SHORT,
        name="down",
    )(info, *shards, down_weight, combine)


FAR = [(0, 2), (2, 0), (1, 3), (3, 1)]
NEAR = [(0, 1), (1, 0), (2, 3), (3, 2)]
MIDDLE = [(1, 2), (2, 1)]
OUTWARD = [(1, 0), (2, 3)]
ACROSS = [(0, 2), (2, 0), (1, 3), (3, 1)]
TWIN = [(0, 1), (1, 0), (2, 3), (3, 2)]


def spread(tokens, wid, hid, *early):
    quarter = tokens.shape[1] // 4
    mine = lax.dynamic_slice_in_dim(tokens, hid * quarter, quarter, axis=1)
    far = lax.ppermute(mine, "wid", FAR)
    near = lax.ppermute(mine, "wid", NEAR)
    near_across = lax.ppermute(near, "hid", ACROSS)
    middle = lax.ppermute(mine, "wid", MIDDLE)
    tokens = after(tokens, near)
    pieces = [tokens[:, q * quarter:(q + 1) * quarter] for q in range(4)]
    far = after(far, near_across, *early, *pieces)
    outer = lax.ppermute(far, "wid", OUTWARD)
    far_across = lax.ppermute(far, "hid", ACROSS)
    third = jnp.where((wid == 1) | (wid == 2), middle, outer)
    third_across = lax.ppermute(third, "hid", ACROSS)
    for piece, across in ((near, near_across), (far, far_across), (third, third_across)):
        pieces += [piece, lax.ppermute(piece, "hid", TWIN), across, lax.ppermute(across, "hid", TWIN)]
    return pieces


def after(value, *done):
    return lax.optimization_barrier((value, *done))[0]


def sparse_device(tokens, gate_weight, up_weight, down_weight, routes, combine):
    experts = gate_weight.shape[0]
    blocks = routes.shape[0]
    rows = combine.shape[0] // blocks
    wid = lax.axis_index("wid")
    hid = lax.axis_index("hid")
    core, x = hid % 2, hid // 2
    info, number = named_pairs(experts, routes)
    count = number[0]
    combine = combine.reshape(blocks, rows, -1)
    pieces = spread(tokens, wid, hid, info, combine)

    def outward(hidden, near, far):
        middle = lax.ppermute(after(hidden, far), "wid", MIDDLE)
        outer = lax.ppermute(far, "wid", OUTWARD)
        return hidden, near, far, middle, outer

    def inward(hidden):
        return hidden, lax.ppermute(hidden, "wid", NEAR), lax.ppermute(hidden, "wid", FAR)

    def shares(parts, blocks):
        at = [2 * (1 - x) + 1 - core, 2 * (1 - x) + core, 2 * x + 1 - core, 2 * x + core]
        return [sum(jnp.where(block == b, part, 0.0) for part, block in zip(parts, blocks)) for b in at]

    def reduced(diagonal, across, twin, own):
        across = across + lax.ppermute(diagonal.astype(BF16), "hid", TWIN).astype(F32)
        own = own + lax.ppermute(twin.astype(BF16), "hid", TWIN).astype(F32)
        arriving = lax.ppermute(across.astype(BF16), "hid", ACROSS)
        return (lax.optimization_barrier(own) + arriving.astype(F32)).astype(BF16)

    most = 4

    def branch(slots, more):
        def run(info, combine, *pieces):
            first, second, parts = [], [], []
            for slot in range(slots + 1):
                if slot < slots:
                    ready = info if slot < 2 else after(info, *first[slot - 2][1:], *parts[-1:])
                    hidden = gate_up(slot, ready, pieces, gate_weight, up_weight)
                    first.append(inward(after(hidden, first[0][2]) if slot == 1 and slots == 2 else hidden))
                if slot >= 1:
                    hidden, near, far = first[slot - 1]
                    far = after(far, parts[-1]) if parts else after(far, near) if slots == 2 else far
                    second.append(outward(hidden, near, far))
                if slot >= 2:
                    ready = after(info, *first[slot - 1][1:], *(first[slot][:1] if slot < slots else ()))
                    parts.append(down(slot - 2, ready, second[slot - 2], combine, down_weight))
            parts.append(down(slots - 1, info, second[slots - 1], combine, down_weight))
            sums = shares(parts, [info[slot, 0] for slot in range(slots)])
            if more:

                def further(state):
                    at, *sums = state
                    one = jnp.concatenate([lax.dynamic_slice_in_dim(info, at, 1, axis=0), info[1:]], axis=0)
                    sent = outward(*inward(gate_up(0, one, pieces, gate_weight, up_weight)))
                    part = down(0, one, sent, combine, down_weight)
                    return at + 1, *[old + new for old, new in zip(sums, shares([part], [one[0, 0]]))]

                _, *sums = lax.while_loop(lambda state: state[0] < count, further, (jnp.int32(slots), *sums))
            return reduced(*sums)

        return run

    branches = [branch(n + 1, False) for n in range(most)] + [branch(most, True)]
    return lax.switch(jnp.minimum(count, most + 1) - 1, branches, info, combine, *pieces)


def dense_device(tokens, gate_weight, up_weight, down_weight, routes, combine):
    experts = gate_weight.shape[0]
    block = combine.shape[0] // routes.shape[0]
    rows_route = jnp.repeat(routes, block, axis=0)
    labels = jnp.arange(experts, dtype=jnp.int32)
    picked = (rows_route[:, :, None] == labels[None, None, :]).astype(F32)
    weights = jnp.sum(combine[:, :, None] * picked, axis=1)
    piece = lax.all_gather(tokens, "wid", axis=0, tiled=True)
    gate = jnp.einsum("td,edf->etf", piece, gate_weight, preferred_element_type=F32)
    upward = jnp.einsum("td,edf->etf", piece, up_weight, preferred_element_type=F32)
    hidden = (jax.nn.silu(gate) * upward).astype(BF16)
    summed = jnp.einsum(
        "etf,efd->etd",
        lax.all_gather(hidden, "wid", axis=2, tiled=True),
        down_weight,
        preferred_element_type=F32,
    )
    partial_value = jnp.sum(jnp.transpose(weights)[:, :, None] * summed, axis=0)
    own_rows = lax.psum_scatter(partial_value, "hid", scatter_dimension=0, tiled=True)
    return own_rows.astype(BF16)


def solution(mesh):
    placed = (
        P(("grp", "wid"), None),
        P(None, None, ("hid", "wid")),
        P(None, None, ("hid", "wid")),
        P(None, "hid", "wid"),
        P("grp", None),
        P("grp", None),
    )

    def program(tokens, gate_weight, up_weight, down_weight, routes, combine):
        blocks = routes.shape[0] // mesh.shape["grp"]
        square = mesh.shape["wid"] == 4 and mesh.shape["hid"] == 4 and blocks == 4
        return jax.shard_map(
            sparse_device if square else dense_device,
            mesh=mesh,
            in_specs=placed,
            out_specs=P(("grp", "hid"), "wid"),
            check_vma=False,
        )(tokens, gate_weight, up_weight, down_weight, routes, combine)

    return program
```
